256 devices in a mesh: dp: 4 (over y_hi, core), context: 16 (over y_lo, z), tensor: 4 (over x).
Axes of the slice: x: 4, y: 4 (y_hi: 2, y_lo: 2; y = y_hi * 2 + y_lo), z: 8, core: 2. Of those that a mesh axis runs over, the one named last changes fastest.
Arguments:
- queries: bfloat16 [8192, 4608], P(('dp', 'context'), 'tensor'), may hold values from -6 to 6
- keys: bfloat16 [8192, 4608], P(('dp', 'context'), 'tensor'), may hold values from -6 to 6
- values: bfloat16 [8192, 4608], P(('dp', 'context'), 'tensor'), may hold values from -7.5 to 7.5
- residual: bfloat16 [8192, 4608], P(('dp', 'context'), 'tensor'), may hold values from -120 to 120
- norm_gain: float32 [4608], P('tensor'), may hold values from 0.1 to 1.9
- routes: int32 [8192, 2], P(('dp', 'context')), may hold values from 0 to 15, all different within a row; in each aligned block of 128 rows (0 to 127, 128 to 255, ...) at most 17 rows name the same one
- route_weight: float32 [8192, 2], P(('dp', 'context')), may hold values from 0.2 to 1
- w_gate: bfloat16 [16, 4608, 6144], P(('dp', 'tensor'), None, 'context'), may hold values from -0.09375 to 0.09375
- w_up: bfloat16 [16, 4608, 6144], P(('dp', 'tensor'), None, 'context'), may hold values from -0.09375 to 0.09375
- w_down: bfloat16 [16, 6144, 4608], P(('dp', 'tensor'), 'context'), may hold values from -0.078125 to 0.078125
- scale_hidden: float32 [16, 2, 6144], P(('dp', 'tensor'), None, 'context'), may hold values from 0.5 to 2
- scale_out: float32 [16, 4608], P(('dp', 'tensor')), may hold values from 0.5 to 2
Outputs:
- output: bfloat16 [8192, 4608], P(('dp', 'context'), 'tensor')
The draws below stay inside these ranges and needn't reach their ends.
Inputs may be any that keep to these rules, and one draw needn't show every extreme that they name: In each aligned block of 128 tokens no expert is named by more than 17 of the block's routes, a bound that some block reaches. Every expert is named somewhere.
All inputs are finite; a program needn't handle non-finite values.
Results may differ from the reference program's by a relative error of at most 0.0095.
Values may be sent and summed in bfloat16 or wider, within the bound.
A program may use at most 128 MiB of HBM per device.

```python
import math
import jax
import jax.numpy as jnp
import numpy as np
from jax import lax

D = 4608
HEADS = 36
HD = 128
EXPERTS = 16
TOP = 2
HID_DEV = 384
TOK_DEV = 128
HID = 6144
CAP = 17
LEN = 2048
SEQS = 4
TOKENS = 8192
N_CONTEXT = 16


def draw_queries(key, part):
    key = jax.random.fold_in(key, 1)
    return jnp.clip(jax.random.normal(key, (TOKENS, D), jnp.float32), -6.0, 6.0).astype(jnp.bfloat16)


def draw_keys(key, part):
    key = jax.random.fold_in(key, 2)
    return jnp.clip(jax.random.normal(key, (TOKENS, D), jnp.float32), -6.0, 6.0).astype(jnp.bfloat16)


def draw_values(key, part):
    key = jax.random.fold_in(key, 4)
    sign_key, noise_key = jax.random.split(key, 2)
    blocks = TOKENS // TOK_DEV
    block_sign = jnp.where(jax.random.bernoulli(sign_key, 0.5, (blocks, 1, D)), 1.5, -1.5).astype(jnp.float32)
    offset = jnp.broadcast_to(block_sign, (blocks, TOK_DEV, D)).reshape(TOKENS, D)
    noise = jnp.clip(jax.random.normal(noise_key, (TOKENS, D), jnp.float32), -6.0, 6.0)
    return (offset + noise).astype(jnp.bfloat16)


def draw_residual(key, part):
    key = jax.random.fold_in(key, 3)
    row_key, col_key, noise_key = jax.random.split(key, 3)
    row_scale = jnp.power(10.0, jax.random.uniform(row_key, (TOKENS, 1), jnp.float32))
    col_scale = jnp.power(10.0, jax.random.uniform(col_key, (1, D), jnp.float32))
    ramp = jnp.power(math.sqrt(3.0), jnp.arange(D, dtype=jnp.float32)[None, :] / D)
    noise = jnp.clip(jax.random.normal(noise_key, (TOKENS, D), jnp.float32), -4.0, 4.0)
    return (0.1 * row_scale * col_scale * ramp * noise).astype(jnp.bfloat16)


def block_levels(rng, dims, cuts, low, largest):
    loudness, own = 1.0, jax.random.fold_in(rng, 6)
    for position, blocks in cuts:
        steps = jnp.exp(jax.random.uniform(jax.random.fold_in(own, position), (blocks,), jnp.float32, low / len(cuts), largest / len(cuts)))
        loudness = loudness * jnp.repeat(steps, dims[position] // blocks).reshape([-1 if axis == position else 1 for axis in range(len(dims))])
    return loudness


def routed_block(own_key, own, number, rows, count, top, limit, skew):
    sequence = jax.random.permutation(own_key, count)
    crowded, ordinary = shares(count, rows * top, limit, skew, True), shares(count, rows * top, limit, skew, False)
    places = jnp.arange(count)

    def named(sizes, rotation):
        used = int((sizes > 0).sum())
        fixed = max(1, used // 4)
        shifted = fixed + (places - fixed + rotation * (used - fixed)) % max(1, count - fixed)
        return jnp.zeros((count,), jnp.int32).at[sequence[jnp.where(places < fixed, places, shifted)]].set(jnp.asarray(sizes, jnp.int32))

    sizes = jnp.where(number % 4 == 0, named(crowded, number // 4), named(ordinary, number - number // 4 - 1))
    mixed = jax.random.permutation(jax.random.fold_in(own, 3), count)
    giver, receiver = mixed[0:count // 2 * 2:2], mixed[1:count // 2 * 2:2]
    slack = jnp.minimum(sizes[giver] - 1, limit - sizes[receiver]) // 2
    slack = jnp.where((giver == sequence[0]) | (receiver == sequence[0]) | (sizes[receiver] == 0), 0, jnp.maximum(slack, 0))
    shifted = jax.random.randint(jax.random.fold_in(own, 4), (count // 2,), 0, 1 << 20) % (slack + 1)
    sizes = sizes.at[giver].add(-shifted).at[receiver].add(shifted)
    members = jnp.searchsorted(jnp.cumsum(sizes), jnp.arange(rows * top), side="right").astype(jnp.int32)
    table = members.reshape(top, rows).T
    table = table[jax.random.permutation(jax.random.fold_in(own, 1), rows)]
    rotation = jax.random.randint(jax.random.fold_in(own, 2), (rows, 1), 0, top)
    return jnp.take_along_axis(table, (jnp.arange(top)[None, :] + rotation) % top, axis=1)


def shares(number_of, total, bound, lean, full):
    weights = [(1 << 20) // math.isqrt(standing ** lean) + 1 for standing in range(1, number_of + 1)]
    largest = bound if full else min(bound, max(-(-total // number_of), total * weights[0] // sum(weights)))
    least = 1 if total - largest >= number_of - 1 else 0
    counts, spare = [largest] + [least] * (number_of - 1), total - largest - least * (number_of - 1)
    while spare > 0:
        candidates = [i for i in range(1, number_of) if counts[i] < largest] or [i for i in range(1, number_of) if counts[i] < bound]
        whole, budget = sum([weights[i] for i in candidates]), spare
        for i in candidates:
            addition = min(bound - counts[i], max(1, budget * weights[i] // whole), spare)
            counts[i] = counts[i] + addition
            spare = spare - addition
    return np.array(counts)


def normal_values(stream_key, shape, spread, most, shards=(), held_as=jnp.bfloat16):
    values = spread * jax.random.normal(stream_key, shape, jnp.float32)
    if shards:
        values = values * block_levels(stream_key, shape, shards, -0.22, 0.18)
    return jnp.clip(values, -most, most).astype(held_as)


def setup_inputs(seed: int = 0) -> dict:
    streams_of = jax.random.split(jax.random.key(seed), 13)
    queries = draw_queries(jax.random.fold_in(streams_of[12], 71), 0)
    keys = draw_keys(jax.random.fold_in(streams_of[12], 71), 0)
    values = draw_values(jax.random.fold_in(streams_of[12], 71), 0)
    residual = draw_residual(jax.random.fold_in(streams_of[12], 71), 0)
    norm_gain = jnp.clip(1.0 + 0.18 * jax.random.normal(streams_of[4], (D,), jnp.float32), 0.1, 1.9)
    routes_keys = jax.random.split(jax.random.fold_in(streams_of[5], 1), TOKENS // TOK_DEV)
    routes_turns = jax.random.permutation(jax.random.fold_in(streams_of[5], 3), TOKENS // TOK_DEV)
    routes = jax.vmap(lambda own, number: routed_block(jax.random.fold_in(streams_of[5], 2), own, number, TOK_DEV, EXPERTS, TOP, CAP, 1))(routes_keys, routes_turns).reshape((TOKENS, TOP))
    route_weight = jnp.clip(0.2 + 0.8 * jax.random.uniform(streams_of[6], (TOKENS, TOP), jnp.float32) ** block_levels(streams_of[6], (TOKENS, TOP), ((0, 64),), -0.2, 0.2), 0.2, 1.0)
    w_gate = normal_values(streams_of[7], (EXPERTS, D, HID), D ** -0.5, 0.09375, ((0, 16), (2, 16)))
    w_up = normal_values(streams_of[8], (EXPERTS, D, HID), D ** -0.5, 0.09375, ((0, 16), (2, 16)))
    w_down = normal_values(streams_of[9], (EXPERTS, HID, D), HID ** -0.5, 0.078125, ((0, 16), (1, 16)))
    scale_hidden = jnp.clip(jnp.exp(math.log(2.0) - 1.3862944 * jax.random.uniform(streams_of[10], (EXPERTS, 2, HID), jnp.float32) ** block_levels(streams_of[10], (EXPERTS, 2, HID), ((0, 16), (2, 16)), -0.2, 0.2)), 0.5, 2.0)
    scale_out = jnp.clip(jnp.exp(math.log(2.0) - 1.3862944 * jax.random.uniform(streams_of[11], (EXPERTS, D), jnp.float32) ** block_levels(streams_of[11], (EXPERTS, D), ((0, 16),), -0.2, 0.2)), 0.5, 2.0)
    return {"queries": queries, "keys": keys, "values": values, "residual": residual, "norm_gain": norm_gain, "routes": routes, "route_weight": route_weight, "w_gate": w_gate, "w_up": w_up, "w_down": w_down, "scale_hidden": scale_hidden, "scale_out": scale_out}


EPS = 1e-06
NEG = -1e+30

def attention(queries, keys, values):
    inv_root = 1.0 / math.sqrt(HD)

    def heads_first(array):
        return array.reshape(SEQS, LEN, HEADS, HD).transpose(0, 2, 1, 3).reshape(SEQS * HEADS, LEN, HD)
    positions = jnp.arange(LEN, dtype=jnp.int32)
    allowed = positions[:, None] >= positions[None, :]

    def one_head(triple):
        query_h, key_h, value_h = triple
        scores = jnp.dot(query_h, key_h.T, preferred_element_type=jnp.float32) * inv_root
        highest = lax.optimization_barrier(jnp.max(jnp.where(allowed, scores, NEG), axis=1, keepdims=True))
        weights = jnp.where(allowed, jnp.exp(scores - highest), 0.0)
        totals = lax.optimization_barrier(jnp.sum(weights, axis=1, keepdims=True))
        blended = jnp.dot(weights.astype(jnp.bfloat16), value_h, preferred_element_type=jnp.float32)
        return (blended / totals).astype(jnp.bfloat16)
    result = lax.map(one_head, (heads_first(queries), heads_first(keys), heads_first(values)))
    return result.reshape(SEQS, HEADS, LEN, HD).transpose(0, 2, 1, 3).reshape(SEQS * LEN, HEADS * HD)

def reference(queries, keys, values, residual, norm_gain, routes, route_weight, w_gate, w_up, w_down, scale_hidden, scale_out):
    attended = attention(queries, keys, values)
    hidden_state = residual.astype(jnp.float32) + lax.optimization_barrier(attended).astype(jnp.float32)
    squares = lax.optimization_barrier(jnp.mean(hidden_state * hidden_state, axis=1, keepdims=True))
    normed = (hidden_state * lax.rsqrt(squares + EPS) * norm_gain[None, :]).astype(jnp.bfloat16)
    blocks = TOKENS // TOK_DEV
    flat = routes.reshape(blocks, TOK_DEV * TOP)
    member = (flat[:, :, None] == jnp.arange(EXPERTS, dtype=jnp.int32)[None, None, :]).astype(jnp.int32)
    ranks = lax.optimization_barrier(jnp.sum((jnp.cumsum(member, axis=1) - member) * member, axis=2)).astype(jnp.int32)
    block_ids = jnp.broadcast_to(jnp.arange(blocks, dtype=jnp.int32)[:, None], flat.shape)
    tokens_of = block_ids * TOK_DEV + jnp.arange(TOK_DEV * TOP, dtype=jnp.int32)[None, :] // TOP
    table = jnp.zeros((EXPERTS, blocks, CAP), jnp.int32).at[flat, block_ids, ranks].set(tokens_of)

    def run_expert(index):
        rows_in = normed[table[index].reshape(-1)]
        gate_val = jnp.dot(rows_in, w_gate[index], preferred_element_type=jnp.float32) * scale_hidden[index, 0][None, :]
        up_val = jnp.dot(rows_in, w_up[index], preferred_element_type=jnp.float32) * scale_hidden[index, 1][None, :]
        activated = (jax.nn.silu(gate_val) * up_val).astype(jnp.bfloat16)
        hidden_blocks = activated.reshape(rows_in.shape[0], N_CONTEXT, HID_DEV)
        down_blocks = w_down[index].reshape(N_CONTEXT, HID_DEV, D)

        def add_block(running, block_no):
            term = jnp.dot(hidden_blocks[:, block_no], down_blocks[block_no], preferred_element_type=jnp.float32).astype(jnp.bfloat16)
            return (running + lax.optimization_barrier(term).astype(jnp.float32), None)
        summed, _ = lax.scan(add_block, jnp.zeros((rows_in.shape[0], D), jnp.float32), jnp.arange(N_CONTEXT, dtype=jnp.int32))
        return (summed * scale_out[index][None, :]).astype(jnp.bfloat16)
    outputs = lax.map(run_expert, jnp.arange(EXPERTS, dtype=jnp.int32))
    picked = outputs[flat.reshape(-1), (block_ids * CAP + ranks).reshape(-1)]
    picked = picked.reshape(TOKENS, TOP, D).astype(jnp.float32)
    routed = lax.optimization_barrier(jnp.sum(picked * route_weight[:, :, None], axis=1))
    return (hidden_state + routed).astype(jnp.bfloat16)
```

```python
import math

import jax
import jax.numpy as jnp
from jax import lax
from jax.experimental import pallas as pl
from jax.experimental.pallas import tpu as pltpu
from jax.sharding import PartitionSpec as P

D = 4608
HD = 128
EXPERTS = 16
TOP = 2
CAP = 17


EPS = 1e-06
NEG = -1e30


N_CTX = 16
HEADS_HERE = 9
MESH = pl.DeviceIdType.MESH
EXP_SCALE = math.log2(math.e) / math.sqrt(HD)


def head_owner(head, core):
    return lax.rem(lax.div(head * N_CTX, HEADS_HERE) + 8 * core, N_CTX)


def attention_kernel(
    q_ref, k_ref, v_ref, out_ref, qs, ks, vs, ob, recv_sem, send_sem, out_send, out_recv
):
    ctx = lax.axis_index("context")
    core = lax.rem(lax.axis_index("dp"), 2)
    rows = q_ref.shape[0]

    barrier = pltpu.get_barrier_semaphore()

    @pl.loop(1, N_CTX)
    def _(step):
        pl.semaphore_signal(
            barrier, inc=1, device_id={"context": lax.rem(ctx + step, N_CTX)}, device_id_type=MESH
        )

    pl.semaphore_wait(barrier, N_CTX - 1)

    my_rows = pl.ds(pl.multiple_of(ctx * rows, rows), rows)
    sources = (k_ref, q_ref, v_ref)
    targets = (ks, qs, vs)

    def scatter(step, start):
        head = lax.rem(ctx + step, HEADS_HERE)
        owner = head_owner(head, core)
        columns = pl.ds(pl.multiple_of(head * HD, HD), HD)
        for index in range(3):
            src = sources[index].at[:, columns]
            dst = targets[index].at[my_rows, :]

            @pl.when(owner != ctx)
            def _():
                copy = pltpu.make_async_remote_copy(
                    src_ref=src,
                    dst_ref=dst,
                    send_sem=send_sem.at[step, index],
                    recv_sem=recv_sem.at[index],
                    device_id={"context": owner},
                    device_id_type=MESH,
                )
                if start:
                    copy.start()
                else:
                    copy.wait_send()

            if start:

                @pl.when(owner == ctx)
                def _():
                    pltpu.make_async_copy(src, dst, recv_sem.at[index]).start()

    @pl.loop(0, HEADS_HERE)
    def _(step):
        scatter(step, True)

    base = lax.rem(ctx + 8 * core, N_CTX)
    my_head = lax.div(base * HEADS_HERE + N_CTX - 1, N_CTX)
    active = jnp.logical_and(
        my_head < HEADS_HERE, lax.div(my_head * N_CTX, HEADS_HERE) == base
    )
    head_columns = pl.ds(pl.multiple_of(lax.rem(my_head, HEADS_HERE) * HD, HD), HD)

    def give(block, start):
        src = ob.at[pl.ds(block * rows, rows), :]
        dst = out_ref.at[:, head_columns]

        @pl.when(ctx != block)
        def _():
            copy = pltpu.make_async_remote_copy(
                src_ref=src,
                dst_ref=dst,
                send_sem=out_send.at[block],
                recv_sem=out_recv,
                device_id={"context": block},
                device_id_type=MESH,
            )
            if start:
                copy.start()
            else:
                copy.wait_send()

        if start:

            @pl.when(ctx == block)
            def _():
                pltpu.make_async_copy(src, dst, out_recv).start()

    @pl.when(active)
    def _():
        for index in range(3):
            pltpu.make_async_copy(targets[index], targets[index], recv_sem.at[index]).wait()
        tile = 2 * rows
        contract = (((1,), (1,)), ((), ()))
        causal = lax.broadcasted_iota(jnp.int32, (tile, tile), 0) >= lax.broadcasted_iota(
            jnp.int32, (tile, tile), 1
        )
        for number in range(N_CTX // 2 - 1, -1, -1):
            low, high = number * tile, (number + 1) * tile
            query = qs[low:high, :]
            own = lax.dot_general(query, ks[low:high, :], contract, preferred_element_type=jnp.float32)
            own = jnp.where(causal, own, NEG)
            top = jnp.max(own, axis=1, keepdims=True)
            if number:
                past = lax.dot_general(
                    query, ks[0:low, :], contract, preferred_element_type=jnp.float32
                )
                top = jnp.maximum(top, jnp.max(past, axis=1, keepdims=True))
            own = jnp.exp2((own - top) * EXP_SCALE)
            total = jnp.sum(own, axis=1, keepdims=True)
            result = jnp.dot(
                own.astype(jnp.bfloat16), vs[low:high, :], preferred_element_type=jnp.float32
            )
            if number:
                past = jnp.exp2((past - top) * EXP_SCALE)
                total = total + jnp.sum(past, axis=1, keepdims=True)
                result = result + jnp.dot(
                    past.astype(jnp.bfloat16), vs[0:low, :], preferred_element_type=jnp.float32
                )
            ob[low:high, :] = (result / total).astype(jnp.bfloat16)
            give(2 * number + 1, True)
            give(2 * number, True)

    @pl.loop(0, HEADS_HERE)
    def _(step):
        scatter(step, False)

    @pl.when(active)
    def _():
        for block in range(N_CTX):
            give(block, False)

    pltpu.make_async_copy(out_ref, out_ref, out_recv).wait()


def attend(queries, keys, values):
    rows, width = queries.shape
    length = rows * N_CTX
    return pl.pallas_call(
        attention_kernel,
        out_shape=jax.ShapeDtypeStruct((rows, width), jnp.bfloat16),
        in_specs=[pl.BlockSpec(memory_space=pl.ANY)] * 3,
        out_specs=pl.BlockSpec(memory_space=pltpu.VMEM),
        scratch_shapes=[
            pltpu.VMEM((length, HD), jnp.bfloat16),
            pltpu.VMEM((length, HD), jnp.bfloat16),
            pltpu.VMEM((length, HD), jnp.bfloat16),
            pltpu.VMEM((length, HD), jnp.bfloat16),
            pltpu.SemaphoreType.DMA((3,)),
            pltpu.SemaphoreType.DMA((HEADS_HERE, 3)),
            pltpu.SemaphoreType.DMA((N_CTX,)),
            pltpu.SemaphoreType.DMA,
        ],
        compiler_params=pltpu.CompilerParams(
            collective_id=0, has_side_effects=True, vmem_limit_bytes=48 * 1024 * 1024
        ),
        cost_estimate=pl.CostEstimate(
            flops=2 * length * length * HD, bytes_accessed=10**6, transcendentals=length * length // 2
        ),
    )(queries, keys, values)


def activate(rows_in, gate_mat, up_mat, gate_scale, up_scale):
    gate_val = jnp.dot(rows_in, gate_mat, preferred_element_type=jnp.float32) * gate_scale
    up_val = jnp.dot(rows_in, up_mat, preferred_element_type=jnp.float32) * up_scale
    return (jax.nn.silu(gate_val) * up_val).astype(jnp.bfloat16)


def local(
    queries,
    keys,
    values,
    residual,
    norm_gain,
    routes,
    route_weight,
    w_gate,
    w_up,
    w_down,
    scale_hidden,
    scale_out,
):
    tok_rows = queries.shape[0]
    n_dp = lax.axis_size("dp")
    n_tensor = lax.axis_size("tensor")
    attended = attend(queries, keys, values)
    hidden_state = residual.astype(jnp.float32) + attended.astype(
        jnp.float32
    )
    square_total = lax.psum(jnp.sum(hidden_state * hidden_state, axis=1), "tensor")
    inverse = lax.rsqrt(square_total / D + EPS)
    normed = (hidden_state * inverse[:, None] * norm_gain[None, :]).astype(jnp.bfloat16)
    flat_routes = routes.reshape(-1)
    route_rows = flat_routes.shape[0]
    member = (flat_routes[:, None] == jnp.arange(EXPERTS, dtype=jnp.int32)[None, :]).astype(
        jnp.int32
    )
    ranks = jnp.sum((jnp.cumsum(member, axis=0) - member) * member, axis=1)
    slot_index = flat_routes * CAP + ranks
    slot_hit = (slot_index[:, None] == jnp.arange(EXPERTS * CAP, dtype=jnp.int32)[None, :]).astype(
        jnp.float32
    )
    token_hit = (
        (jnp.arange(route_rows, dtype=jnp.int32) // TOP)[:, None]
        == jnp.arange(tok_rows, dtype=jnp.int32)[None, :]
    ).astype(jnp.float32)
    dispatch = jnp.dot(slot_hit.T, token_hit, precision=lax.Precision.HIGHEST).astype(jnp.bfloat16)
    combine = jnp.dot(
        token_hit.T, slot_hit * route_weight.reshape(-1)[:, None], precision=lax.Precision.HIGHEST
    )
    tensor_pos = lax.axis_index("tensor")
    widened = lax.all_gather(normed, "tensor", axis=1, tiled=True)
    own_slots = lax.dynamic_index_in_dim(
        dispatch.reshape(n_dp, n_tensor, CAP, tok_rows), tensor_pos, axis=1, keepdims=False
    ).reshape(n_dp * CAP, tok_rows)
    outgoing = jnp.dot(own_slots, widened, preferred_element_type=jnp.float32).astype(jnp.bfloat16)
    expert_rows = lax.all_to_all(outgoing, "dp", split_axis=0, concat_axis=0, tiled=True)
    activated = activate(
        lax.all_gather(expert_rows, "context", axis=0, tiled=True),
        w_gate[0],
        w_up[0],
        scale_hidden[0, 0][None, :],
        scale_hidden[0, 1][None, :],
    )
    summed = lax.psum_scatter(
        jnp.dot(activated, w_down[0], preferred_element_type=jnp.float32).astype(jnp.bfloat16),
        "context",
        scatter_dimension=0,
        tiled=True,
    ).astype(jnp.float32)
    expert_out = (summed * scale_out[0][None, :]).astype(jnp.bfloat16)
    returned = lax.all_to_all(expert_out, "dp", split_axis=0, concat_axis=0, tiled=True)
    own_combine = lax.dynamic_index_in_dim(
        combine.reshape(tok_rows, n_dp, n_tensor, CAP), tensor_pos, axis=2, keepdims=False
    ).reshape(tok_rows, n_dp * CAP)
    partial_full = jnp.dot(
        own_combine, returned.astype(jnp.float32), precision=lax.Precision.HIGHEST
    )
    routed = lax.psum_scatter(
        partial_full.astype(jnp.bfloat16), "tensor", scatter_dimension=1, tiled=True
    ).astype(jnp.float32)
    return (hidden_state + routed).astype(jnp.bfloat16)


def solution(mesh):
    in_specs = (
        P(("dp", "context"), "tensor"),
        P(("dp", "context"), "tensor"),
        P(("dp", "context"), "tensor"),
        P(("dp", "context"), "tensor"),
        P("tensor"),
        P(("dp", "context"), None),
        P(("dp", "context"), None),
        P(("dp", "tensor"), None, "context"),
        P(("dp", "tensor"), None, "context"),
        P(("dp", "tensor"), "context", None),
        P(("dp", "tensor"), None, "context"),
        P(("dp", "tensor"), None),
    )
    out_specs = P(("dp", "context"), "tensor")
    return jax.shard_map(local, mesh=mesh, in_specs=in_specs, out_specs=out_specs, check_vma=False)
```

```python
import math

import jax
import jax.numpy as jnp
from jax import lax
from jax.experimental import pallas as pl
from jax.experimental.pallas import tpu as pltpu
from jax.sharding import PartitionSpec as P

D = 4608
HD = 128
EXPERTS = 16
EPS = 1e-06
NEG = -1e30
N_CTX = 16
HEADS_HERE = 9
MESH = pl.DeviceIdType.MESH
EXP_SCALE = math.log2(math.e) / math.sqrt(HD)


def head_owner(head, core):
    return lax.rem(lax.div(head * N_CTX, HEADS_HERE) + 8 * core, N_CTX)


def attention_kernel(
    q_ref,
    k_ref,
    v_ref,
    gate_ref,
    out_ref,
    gate_out,
    qs,
    ks,
    vs,
    ob,
    recv_sem,
    send_sem,
    out_send,
    out_recv,
    gate_send,
    gate_recv,
):
    ctx = lax.axis_index("context")
    dp = lax.axis_index("dp")
    core = lax.rem(dp, 2)
    swapping = core != lax.div(ctx, N_CTX // 2)
    diagonal = {"dp": dp + 1 - 2 * core, "context": lax.rem(ctx + N_CTX // 2, N_CTX)}
    rows = q_ref.shape[0]

    barrier = pltpu.get_barrier_semaphore()

    @pl.loop(1, N_CTX)
    def _(step):
        pl.semaphore_signal(
            barrier, inc=1, device_id={"context": lax.rem(ctx + step, N_CTX)}, device_id_type=MESH
        )

    pl.semaphore_signal(barrier, inc=1, device_id=diagonal, device_id_type=MESH)
    pl.semaphore_wait(barrier, N_CTX)
    swap = pltpu.make_async_remote_copy(
        src_ref=gate_ref,
        dst_ref=gate_out,
        send_sem=gate_send,
        recv_sem=gate_recv,
        device_id=diagonal,
        device_id_type=MESH,
    )

    my_rows = pl.ds(pl.multiple_of(ctx * rows, rows), rows)
    sources = (k_ref, q_ref, v_ref)
    targets = (ks, qs, vs)

    def scatter(step, start):
        head = lax.rem(ctx + step, HEADS_HERE)
        owner = head_owner(head, core)
        columns = pl.ds(pl.multiple_of(head * HD, HD), HD)
        for index in range(3):
            src = sources[index].at[:, columns]
            dst = targets[index].at[my_rows, :]

            @pl.when(owner != ctx)
            def _():
                copy = pltpu.make_async_remote_copy(
                    src_ref=src,
                    dst_ref=dst,
                    send_sem=send_sem.at[step, index],
                    recv_sem=recv_sem.at[index],
                    device_id={"context": owner},
                    device_id_type=MESH,
                )
                if start:
                    copy.start()
                else:
                    copy.wait_send()

            if start:

                @pl.when(owner == ctx)
                def _():
                    pltpu.make_async_copy(src, dst, recv_sem.at[index]).start()

    @pl.loop(0, HEADS_HERE)
    def _(step):
        scatter(step, True)

    @pl.when(swapping)
    def _():
        swap.start()

    base = lax.rem(ctx + 8 * core, N_CTX)
    my_head = lax.div(base * HEADS_HERE + N_CTX - 1, N_CTX)
    active = jnp.logical_and(
        my_head < HEADS_HERE, lax.div(my_head * N_CTX, HEADS_HERE) == base
    )
    head_columns = pl.ds(pl.multiple_of(lax.rem(my_head, HEADS_HERE) * HD, HD), HD)

    def give(block, start):
        src = ob.at[pl.ds(block * rows, rows), :]
        dst = out_ref.at[:, head_columns]

        @pl.when(ctx != block)
        def _():
            copy = pltpu.make_async_remote_copy(
                src_ref=src,
                dst_ref=dst,
                send_sem=out_send.at[block],
                recv_sem=out_recv,
                device_id={"context": block},
                device_id_type=MESH,
            )
            if start:
                copy.start()
            else:
                copy.wait_send()

        if start:

            @pl.when(ctx == block)
            def _():
                pltpu.make_async_copy(src, dst, out_recv).start()

    @pl.when(active)
    def _():
        for index in range(3):
            pltpu.make_async_copy(targets[index], targets[index], recv_sem.at[index]).wait()
        tile = 2 * rows
        contract = (((1,), (1,)), ((), ()))
        causal = lax.broadcasted_iota(jnp.int32, (tile, tile), 0) >= lax.broadcasted_iota(
            jnp.int32, (tile, tile), 1
        )
        for number in range(N_CTX // 2 - 1, -1, -1):
            low, high = number * tile, (number + 1) * tile
            query = qs[low:high, :]
            own = lax.dot_general(query, ks[low:high, :], contract, preferred_element_type=jnp.float32)
            own = jnp.where(causal, own, NEG)
            top = jnp.max(own, axis=1, keepdims=True)
            if number:
                past = lax.dot_general(
                    query, ks[0:low, :], contract, preferred_element_type=jnp.float32
                )
                top = jnp.maximum(top, jnp.max(past, axis=1, keepdims=True))
            own = jnp.exp2((own - top) * EXP_SCALE)
            total = jnp.sum(own, axis=1, keepdims=True)
            result = jnp.dot(
                own.astype(jnp.bfloat16), vs[low:high, :], preferred_element_type=jnp.float32
            )
            if number:
                past = jnp.exp2((past - top) * EXP_SCALE)
                total = total + jnp.sum(past, axis=1, keepdims=True)
                result = result + jnp.dot(
                    past.astype(jnp.bfloat16), vs[0:low, :], preferred_element_type=jnp.float32
                )
            ob[low:high, :] = (result / total).astype(jnp.bfloat16)
            give(2 * number + 1, True)
            give(2 * number, True)

    @pl.loop(0, HEADS_HERE)
    def _(step):
        scatter(step, False)

    @pl.when(active)
    def _():
        for block in range(N_CTX):
            give(block, False)

    pltpu.make_async_copy(out_ref, out_ref, out_recv).wait()

    @pl.when(swapping)
    def _():
        swap.wait()


def attend(queries, keys, values, w_gate):
    rows, width = queries.shape
    length = rows * N_CTX
    return pl.pallas_call(
        attention_kernel,
        out_shape=(
            jax.ShapeDtypeStruct((rows, width), jnp.bfloat16),
            jax.ShapeDtypeStruct(w_gate.shape, jnp.bfloat16),
        ),
        in_specs=[pl.BlockSpec(memory_space=pl.ANY)] * 4,
        out_specs=(pl.BlockSpec(memory_space=pltpu.VMEM), pl.BlockSpec(memory_space=pl.ANY)),
        scratch_shapes=[
            pltpu.VMEM((length, HD), jnp.bfloat16),
            pltpu.VMEM((length, HD), jnp.bfloat16),
            pltpu.VMEM((length, HD), jnp.bfloat16),
            pltpu.VMEM((length, HD), jnp.bfloat16),
            pltpu.SemaphoreType.DMA((3,)),
            pltpu.SemaphoreType.DMA((HEADS_HERE, 3)),
            pltpu.SemaphoreType.DMA((N_CTX,)),
            pltpu.SemaphoreType.DMA,
            pltpu.SemaphoreType.DMA,
            pltpu.SemaphoreType.DMA,
        ],
        compiler_params=pltpu.CompilerParams(
            collective_id=0, has_side_effects=True, vmem_limit_bytes=48 * 1024 * 1024
        ),
        cost_estimate=pl.CostEstimate(
            flops=2 * length * length * HD, bytes_accessed=10**6, transcendentals=length * length // 2
        ),
    )(queries, keys, values, w_gate)


MAIN = 16
TILE_ROWS = 16
SLOT = 64
OVER = 256
GROUP = 16
N_Z = 8
OWN, SIB_OWN = 0, 1


def major(k):
    return 14 if k == 4 else 4 * k - 2


def minor(k):
    return 4 * k - 1


def twin(slot):
    return slot + 1 if slot in (0, 14) else slot + 2


CARRIED = [OWN] + [s for k in (1, 2, 3) for s in (major(k), minor(k))] + [major(4)]
STEPS = [(0, 2), (2, 4), (6, 4), (10, 4), (14, 2)]


def arrived(ref, sem):
    pltpu.make_async_copy(ref, ref, sem).wait()


def one_hot(hit):
    return jnp.where(hit, 1.0, 0.0).astype(jnp.bfloat16)


def exact_dot(left, right):
    return jnp.dot(left, right, preferred_element_type=jnp.float32)


def iotas(rows, columns):
    return (
        lax.broadcasted_iota(jnp.int32, (rows, columns), 0),
        lax.broadcasted_iota(jnp.int32, (rows, columns), 1),
    )


def expert_kernel(
    residual_ref,
    attended_ref,
    gain_ref,
    routes_ref,
    routes_t_ref,
    weight_ref,
    gate_own,
    gate_swapped,
    up_own,
    down_own,
    wide_own,
    tall_own,
    out_ref,
    xm,
    xo,
    ym,
    yo,
    sib_m,
    sib_o,
    rxa_m,
    rxa_o,
    rxb_m,
    rxb_o,
    w1,
    wd,
    wide,
    tall,
    act,
    hid,
    hidden,
    disp_m,
    disp_o,
    eo_m,
    eo_o,
    ret_m,
    ret_o,
    over_x,
    over_y,
    spread,
    gather,
    squares,
    w_recv,
    w_send,
    sq_recv,
    sq_send,
    disp_recv,
    disp_send,
    aga_recv,
    aga_send,
    agb_recv,
    agb_send,
    sibx_recv,
    sibx_send,
    siby_recv,
    siby_send,
    rsa_recv,
    rsa_send,
    rsb_recv,
    rsb_send,
    ret_recv,
    ret_send,
):
    dp, ctx, tensor = lax.axis_index("dp"), lax.axis_index("context"), lax.axis_index("tensor")
    core, y_hi = lax.rem(dp, 2), lax.div(dp, 2)
    z, y_lo = lax.rem(ctx, N_Z), lax.div(ctx, N_Z)
    sign = 1 - 2 * core
    place = y_hi * 2 + y_lo
    rank = place * 4 + tensor
    rows, quarter = residual_ref.shape
    width = xm.shape[1]
    hid_dev = wd.shape[0]

    def member(number):
        other = lax.div(number, 4)
        return {
            "dp": lax.div(other, 2) * 2 + core,
            "context": lax.rem(other, 2) * N_Z + z,
            "tensor": lax.rem(number, 4),
        }

    ahead = {"context": y_lo * N_Z + lax.rem(z + sign + N_Z, N_Z)}
    behind = {"context": y_lo * N_Z + lax.rem(z - sign + N_Z, N_Z)}
    sibling = {"dp": y_hi * 2 + 1 - core}
    diagonal = {"dp": y_hi * 2 + 1 - core, "context": (1 - y_lo) * N_Z + z}

    barrier = pltpu.get_barrier_semaphore()
    for other in (ahead, behind, sibling, diagonal):
        pl.semaphore_signal(barrier, inc=1, device_id=other, device_id_type=MESH)

    @pl.loop(1, GROUP)
    def _(step):
        pl.semaphore_signal(
            barrier, inc=1, device_id=member(lax.rem(rank + step, GROUP)), device_id_type=MESH
        )

    pl.semaphore_wait(barrier, GROUP + 3)

    pending = []

    def send(src, dst, send_sem, recv_sem, device):
        copy = pltpu.make_async_remote_copy(
            src_ref=src,
            dst_ref=dst,
            send_sem=send_sem,
            recv_sem=recv_sem,
            device_id=device,
            device_id_type=MESH,
        )
        copy.start()
        pending.append(copy)

    swapping = core != y_lo
    up_part = w1.at[:, pl.ds(hid_dev, hid_dev)]
    gate_part = w1.at[:, pl.ds(0, hid_dev)]
    moved = ((up_own, up_part), (down_own, wd), (wide_own, wide), (tall_own, tall))

    def swap(index):
        return pltpu.make_async_remote_copy(
            src_ref=moved[index][0],
            dst_ref=moved[index][1],
            send_sem=w_send.at[index],
            recv_sem=w_recv.at[index],
            device_id=diagonal,
            device_id_type=MESH,
        )

    @pl.when(swapping)
    def _():
        for index in (2, 3, 0, 1):
            swap(index).start()
        pltpu.make_async_copy(gate_swapped, gate_part, w_recv.at[4]).start()

    @pl.when(jnp.logical_not(swapping))
    def _():
        for index in (2, 3, 0, 1):
            pltpu.make_async_copy(moved[index][0], moved[index][1], w_recv.at[index]).start()
        pltpu.make_async_copy(gate_own, gate_part, w_recv.at[4]).start()

    state = residual_ref[...].astype(jnp.float32) + attended_ref[...].astype(jnp.float32)
    hidden[...] = state
    own_squares = jnp.sum(state * state, axis=1, keepdims=True)
    squares[tensor] = jnp.broadcast_to(own_squares, (rows, rows)).T[0:8, :]

    def tell(step):
        peer = lax.rem(tensor + step, 4)
        return pltpu.make_async_remote_copy(
            src_ref=squares.at[tensor],
            dst_ref=squares.at[tensor],
            send_sem=sq_send.at[peer],
            recv_sem=sq_recv.at[tensor],
            device_id={"tensor": peer},
            device_id_type=MESH,
        )

    for step in (1, 2, 3):
        tell(step).start()

    row, col = iotas(EXPERTS, rows)
    named = jnp.logical_or(row == routes_t_ref[0:1, :], row == routes_t_ref[1:2, :])
    first, second = iotas(rows, rows)
    ranks = exact_dot(one_hot(named), one_hot(first < second))
    ranks = jnp.where(named, ranks, -1.0)
    row, col = iotas(EXPERTS * MAIN, EXPERTS)
    widened = exact_dot(one_hot((row >> 4) == col), ranks.astype(jnp.bfloat16))
    row, col = iotas(EXPERTS * MAIN, rows)
    pick_main = one_hot(widened == (row & 15).astype(jnp.float32))
    pick_over = one_hot(ranks == float(MAIN))

    for step in (1, 2, 3):
        peer = lax.rem(tensor + step, 4)
        arrived(squares.at[peer], sq_recv.at[peer])
    total = squares[0] + squares[1] + squares[2] + squares[3]
    inverse = lax.rsqrt(total / D + EPS)
    inverse = jnp.broadcast_to(inverse[0:1, :], (rows, rows)).T[:, 0:1]
    normed = (hidden[...] * inverse * gain_ref[...]).astype(jnp.bfloat16)
    disp_m[...] = exact_dot(pick_main, normed).astype(jnp.bfloat16)
    overflow = exact_dot(pick_over, normed).astype(jnp.bfloat16)
    pieces = quarter // HD
    stacked = jnp.concatenate(
        [overflow[:, n * HD : (n + 1) * HD] for n in range(pieces)], axis=0
    )
    row, col = iotas(EXPERTS * TILE_ROWS, EXPERTS * pieces)
    shuffle = one_hot((((col & 15) << 4) | (col >> 4)) == row)
    disp_o[...] = exact_dot(shuffle, stacked).astype(jnp.bfloat16)

    def rows_of(number):
        return pl.ds(pl.multiple_of(number * TILE_ROWS, TILE_ROWS), TILE_ROWS)

    def columns_of(number):
        return pl.ds(pl.multiple_of(number * quarter, quarter), quarter)

    def dispatch(step):
        other = lax.rem(rank + step, GROUP)
        pairs = (
            (disp_m.at[rows_of(other), :], xm.at[rows_of(place), columns_of(tensor)]),
            (disp_o.at[rows_of(other), :], xo.at[rows_of(rank), :]),
        )
        return [
            pltpu.make_async_remote_copy(
                src_ref=src,
                dst_ref=dst,
                send_sem=disp_send.at[step, index],
                recv_sem=disp_recv.at[index],
                device_id=member(other),
                device_id_type=MESH,
            )
            for index, (src, dst) in enumerate(pairs)
        ]

    pltpu.make_async_copy(
        disp_m.at[rows_of(rank), :], xm.at[rows_of(place), columns_of(tensor)], disp_recv.at[0]
    ).start()
    pltpu.make_async_copy(
        disp_o.at[rows_of(rank), :], xo.at[rows_of(rank), :], disp_recv.at[1]
    ).start()

    @pl.loop(1, GROUP)
    def _(step):
        for copy in dispatch(step):
            copy.start()

    row, col = iotas(36 * 16, 4 * OVER)
    chunk, inside = col >> 8, col & 255
    source, part, piece = inside >> 6, (inside >> 4) & 3, inside & 15
    goal = (part * pieces + piece) * 16 + chunk * 4 + source
    spread[...] = one_hot(jnp.logical_and(piece < pieces, goal == row))
    row, col = iotas(4 * OVER, 36 * 16)
    chunk, inside = row >> 8, row & 255
    source, part, piece = inside >> 6, (inside >> 4) & 3, inside & 15
    goal = (part * pieces + piece) * 16 + chunk * 4 + source
    gather[...] = one_hot(jnp.logical_and(piece < pieces, goal == col))

    def main(slot):
        return pl.ds(slot * SLOT, SLOT)

    def over(slot):
        return pl.ds(slot * OVER, OVER)

    def pass_on(slot, goal, send_sem, recv_sem, number, device):
        send(xm.at[main(slot), :], xm.at[main(goal), :], send_sem.at[number, 0], recv_sem.at[number, 0], device)
        send(xo.at[over(slot), :], xo.at[over(goal), :], send_sem.at[number, 1], recv_sem.at[number, 1], device)

    def landed(slot, recv_sem, number):
        arrived(xm.at[main(slot), :], recv_sem.at[number, 0])
        arrived(xo.at[over(slot), :], recv_sem.at[number, 1])

    def share(slot):
        pass_on(slot, twin(slot), sibx_send, sibx_recv, CARRIED.index(slot), sibling)

    arrived(xm.at[main(OWN), :], disp_recv.at[0])
    arrived(xo.at[over(OWN), :], disp_recv.at[1])
    pass_on(OWN, major(1), aga_send, aga_recv, 0, ahead)
    pass_on(OWN, minor(1), agb_send, agb_recv, 0, behind)
    share(OWN)
    for k in (1, 2, 3):
        landed(major(k), aga_recv, k - 1)
        pass_on(major(k), major(k + 1), aga_send, aga_recv, k, ahead)
        share(major(k))
        landed(minor(k), agb_recv, k - 1)
        if k < 3:
            pass_on(minor(k), minor(k + 1), agb_send, agb_recv, k, behind)
        share(minor(k))

    def fetch_shared(step):
        low, count = STEPS[step]
        for slot in CARRIED:
            if low <= slot < low + count:
                landed(twin(slot), sibx_recv, CARRIED.index(slot))

    def step_rows(step):
        return STEPS[step][1] * SLOT

    def hidden_part(step):
        low, count = STEPS[step]
        size = step_rows(step)
        tiles = xo[low * OVER : (low + count) * OVER, :]
        stack = exact_dot(spread[:, 0 : count * OVER], tiles).astype(jnp.bfloat16)
        for n in range(36):
            over_x[:, n * HD : (n + 1) * HD] = stack[n * 16 : (n + 1) * 16, :]

        @pl.loop(0, 3)
        def _(n):
            lanes = pl.ds(pl.multiple_of(n * 256, 256), 256)
            rows_in = jnp.concatenate([xm[low * SLOT : low * SLOT + size, :], over_x[...]], axis=0)
            hid[0 : size + 16, lanes] = exact_dot(rows_in, w1[:, lanes])

        for n in range(hid_dev // HD):
            lanes = slice(n * HD, (n + 1) * HD)
            gate = hid[0 : size + 16, lanes] * tall[n : n + 1, :]
            up = hid[0 : size + 16, hid_dev + n * HD : hid_dev + (n + 1) * HD] * tall[n + 3 : n + 4, :]
            act[step * 272 : step * 272 + size + 16, lanes] = (
                gate / (1.0 + jnp.exp(-gate)) * up
            ).astype(jnp.bfloat16)

    def down_part(step):
        low, count = STEPS[step]
        size = step_rows(step)

        @pl.loop(0, width // 512)
        def _(n):
            lanes = pl.ds(pl.multiple_of(n * 512, 512), 512)
            result = exact_dot(act[step * 272 : step * 272 + size + 16, :], wd[:, lanes])
            result = result.astype(jnp.bfloat16)
            ym[low * SLOT : low * SLOT + size, lanes] = result[0:size, :]
            over_y[:, lanes] = result[size:, :]

        stack = jnp.concatenate([over_y[:, n * HD : (n + 1) * HD] for n in range(36)], axis=0)
        yo[low * OVER : (low + count) * OVER, :] = exact_dot(
            gather[0 : count * OVER, :], stack
        ).astype(jnp.bfloat16)
        for slot in CARRIED:
            if low <= slot < low + count:
                number = CARRIED.index(slot)
                other = twin(slot)
                send(ym.at[main(other), :], sib_m.at[number], siby_send.at[number, 0], siby_recv.at[number, 0], sibling)
                send(yo.at[over(other), :], sib_o.at[number], siby_send.at[number, 1], siby_recv.at[number, 1], sibling)

    arrived(gate_part, w_recv.at[4])
    arrived(up_part, w_recv.at[0])
    arrived(wide, w_recv.at[2])
    arrived(tall, w_recv.at[3])
    for step in (0, 1, 2, 3):
        fetch_shared(step)
        hidden_part(step)
    landed(major(4), aga_recv, 3)
    share(major(4))
    fetch_shared(4)
    hidden_part(4)
    arrived(wd, w_recv.at[1])

    def add_up(slot, extras):
        number = CARRIED.index(slot)
        arrived(sib_m.at[number], siby_recv.at[number, 0])
        arrived(sib_o.at[number], siby_recv.at[number, 1])

        def summed(own, others):
            value = own.astype(jnp.float32)
            for other in others:
                value = value + other.astype(jnp.float32)
            return value

        def block(lanes):
            return summed(
                ym[main(slot), lanes],
                [sib_m[number, :, lanes]] + [ref[place, :, lanes] for ref, _, place in extras],
            )

        tiles = summed(
            yo[over(slot), :], [sib_o[number]] + [ref[place] for _, ref, place in extras]
        )
        return block, tiles

    def hop(slot, extras, goal_m, goal_o, send_sem, recv_sem, number, device):
        for ref_m, ref_o, place, sems in extras:
            arrived(ref_m.at[place], sems.at[place, 0])
            arrived(ref_o.at[place], sems.at[place, 1])
        block, tiles = add_up(slot, [e[:3] for e in extras])

        @pl.loop(0, width // 512)
        def _(n):
            lanes = pl.ds(pl.multiple_of(n * 512, 512), 512)
            ym[main(slot), lanes] = block(lanes).astype(jnp.bfloat16)

        send(ym.at[main(slot), :], goal_m.at[number], send_sem.at[number, 0], recv_sem.at[number, 0], device)
        yo[over(slot), :] = tiles.astype(jnp.bfloat16)
        send(yo.at[over(slot), :], goal_o.at[number], send_sem.at[number, 1], recv_sem.at[number, 1], device)

    def hop_a(k):
        extras = [(rxa_m, rxa_o, k, rsa_recv)] if k < 4 else []
        hop(major(k), extras, rxa_m, rxa_o, rsa_send, rsa_recv, k - 1, behind)

    def hop_b(k):
        extras = [(rxb_m, rxb_o, k, rsb_recv)] if k < 3 else []
        hop(minor(k), extras, rxb_m, rxb_o, rsb_send, rsb_recv, k - 1, ahead)

    down_part(4)
    hop_a(4)
    down_part(3)
    hop_b(3)
    down_part(2)
    down_part(1)
    down_part(0)
    hop_a(3)
    hop_b(2)
    hop_a(2)
    hop_b(1)
    hop_a(1)
    last = [(rxb_m, rxb_o, 0, rsb_recv), (rxa_m, rxa_o, 0, rsa_recv)]
    for ref_m, ref_o, spot, sems in last:
        arrived(ref_m.at[spot], sems.at[spot, 0])
        arrived(ref_o.at[spot], sems.at[spot, 1])
    block, tiles = add_up(OWN, [e[:3] for e in last])

    @pl.loop(0, width // 512)
    def _(n):
        lanes = pl.ds(pl.multiple_of(n * 512, 512), 512)
        eo_m[:, lanes] = (block(lanes) * wide[0:1, lanes]).astype(jnp.bfloat16)

    for n in range(4):
        eo_o[n * 64 : (n + 1) * 64, :] = (tiles[n * 64 : (n + 1) * 64, :] * tall[8:72, :]).astype(
            jnp.bfloat16
        )

    def give_back(step):
        other = lax.rem(rank + step, GROUP)
        to_place, to_part = lax.div(other, 4), lax.rem(other, 4)
        pairs = (
            (eo_m.at[rows_of(to_place), columns_of(to_part)], ret_m.at[rows_of(rank), :]),
            (eo_o.at[rows_of(other), :], ret_o.at[rows_of(rank), :]),
        )
        return [
            pltpu.make_async_remote_copy(
                src_ref=src,
                dst_ref=dst,
                send_sem=ret_send.at[step, index],
                recv_sem=ret_recv.at[index],
                device_id=member(other),
                device_id_type=MESH,
            )
            for index, (src, dst) in enumerate(pairs)
        ]

    pltpu.make_async_copy(
        eo_m.at[rows_of(place), columns_of(tensor)], ret_m.at[rows_of(rank), :], ret_recv.at[0]
    ).start()
    pltpu.make_async_copy(
        eo_o.at[rows_of(rank), :], ret_o.at[rows_of(rank), :], ret_recv.at[1]
    ).start()

    @pl.loop(1, GROUP)
    def _(step):
        for copy in give_back(step):
            copy.start()

    expert_id = iotas(rows, EXPERTS)[1]
    hits = [expert_id == routes_ref[:, k : k + 1] for k in range(2)]
    first, second = iotas(rows, rows)
    both = one_hot(jnp.logical_or(hits[0], hits[1]))
    token_ranks = exact_dot(one_hot(second < first), both)
    row, col = iotas(EXPERTS, EXPERTS * MAIN)
    expand = one_hot((col >> 4) == row)
    slot_rank = (iotas(rows, EXPERTS * MAIN)[1] & 15).astype(jnp.float32)
    selects = []
    for k in range(2):
        own_ranks = jnp.where(hits[k], token_ranks, -1.0)
        wide_ranks = exact_dot(own_ranks.astype(jnp.bfloat16), expand)
        selects.append((one_hot(wide_ranks == slot_rank), one_hot(own_ranks == float(MAIN))))
    row, col = iotas(EXPERTS * pieces, EXPERTS * TILE_ROWS)
    unshuffle = one_hot((((row & 15) << 4) | (row >> 4)) == col)

    arrived(ret_m, ret_recv.at[0])
    arrived(ret_o, ret_recv.at[1])
    back = exact_dot(unshuffle, ret_o[...]).astype(jnp.bfloat16)
    back = jnp.concatenate(
        [back[n * EXPERTS : (n + 1) * EXPERTS, :] for n in range(pieces)], axis=1
    )
    routed = jnp.zeros((rows, quarter), jnp.float32)
    for k in range(2):
        picked = exact_dot(selects[k][0], ret_m[...]) + exact_dot(selects[k][1], back)
        routed = routed + picked * weight_ref[:, k : k + 1]
    out_ref[...] = (hidden[...] + routed).astype(jnp.bfloat16)

    for copy in pending:
        copy.wait_send()
    for step in (1, 2, 3):
        tell(step).wait_send()

    @pl.loop(1, GROUP)
    def _(step):
        for copy in dispatch(step) + give_back(step):
            copy.wait_send()

    @pl.when(swapping)
    def _():
        for index in range(4):
            swap(index).wait_send()


def experts(
    residual, attended, norm_gain, routes, route_weight, gate_swapped, w_gate, w_up, w_down, scale_hidden, scale_out
):
    rows, quarter = residual.shape
    width, hid_dev = w_gate.shape
    wide = jnp.broadcast_to(scale_out, (8, width))
    pieces = quarter // HD
    tall = jnp.concatenate(
        [
            jnp.pad(scale_hidden.reshape(2 * hid_dev // HD, HD), ((0, 2), (0, 0))),
            jnp.pad(scale_out.reshape(4, pieces, HD), ((0, 0), (0, 16 - pieces), (0, 0))).reshape(64, HD),
        ],
        axis=0,
    )
    vmem = pl.BlockSpec(memory_space=pltpu.VMEM)
    hbm = pl.BlockSpec(memory_space=pl.ANY)
    half = jnp.bfloat16
    dma = pltpu.SemaphoreType.DMA
    return pl.pallas_call(
        expert_kernel,
        out_shape=jax.ShapeDtypeStruct((rows, quarter), half),
        in_specs=[vmem] * 6 + [hbm] * 6,
        out_specs=vmem,
        scratch_shapes=[
            pltpu.VMEM((16 * SLOT, width), half),
            pltpu.VMEM((16 * OVER, HD), half),
            pltpu.VMEM((16 * SLOT, width), half),
            pltpu.VMEM((16 * OVER, HD), half),
            pltpu.VMEM((8, SLOT, width), half),
            pltpu.VMEM((8, OVER, HD), half),
            pltpu.VMEM((4, SLOT, width), half),
            pltpu.VMEM((4, OVER, HD), half),
            pltpu.VMEM((3, SLOT, width), half),
            pltpu.VMEM((3, OVER, HD), half),
            pltpu.VMEM((width, 2 * hid_dev), half),
            pltpu.VMEM((hid_dev, width), half),
            pltpu.VMEM((8, width), jnp.float32),
            pltpu.VMEM((72, HD), jnp.float32),
            pltpu.VMEM((5 * 272, hid_dev), half),
            pltpu.VMEM((272, 2 * hid_dev), jnp.float32),
            pltpu.VMEM((rows, quarter), jnp.float32),
            pltpu.VMEM((EXPERTS * MAIN, quarter), half),
            pltpu.VMEM((EXPERTS * TILE_ROWS, HD), half),
            pltpu.VMEM((SLOT, width), half),
            pltpu.VMEM((OVER, HD), half),
            pltpu.VMEM((EXPERTS * MAIN, quarter), half),
            pltpu.VMEM((EXPERTS * TILE_ROWS, HD), half),
            pltpu.VMEM((16, width), half),
            pltpu.VMEM((16, width), half),
            pltpu.VMEM((36 * 16, 4 * OVER), half),
            pltpu.VMEM((4 * OVER, 36 * 16), half),
            pltpu.VMEM((4, 8, rows), jnp.float32),
            dma((5,)),
            dma((4,)),
            dma((4,)),
            dma((4,)),
            dma((2,)),
            dma((GROUP, 2)),
            dma((4, 2)),
            dma((4, 2)),
            dma((3, 2)),
            dma((3, 2)),
            dma((8, 2)),
            dma((8, 2)),
            dma((8, 2)),
            dma((8, 2)),
            dma((4, 2)),
            dma((4, 2)),
            dma((3, 2)),
            dma((3, 2)),
            dma((2,)),
            dma((GROUP, 2)),
        ],
        compiler_params=pltpu.CompilerParams(
            collective_id=1, has_side_effects=True, vmem_limit_bytes=60 * 1024 * 1024
        ),
        cost_estimate=pl.CostEstimate(
            flops=6 * 1088 * width * hid_dev, bytes_accessed=12 * 10**6, transcendentals=10**6
        ),
    )(
        residual,
        attended,
        norm_gain.reshape(1, quarter),
        routes,
        routes.T,
        route_weight,
        w_gate,
        gate_swapped,
        w_up,
        w_down,
        wide,
        tall,
    )


def local(
    queries,
    keys,
    values,
    residual,
    norm_gain,
    routes,
    route_weight,
    w_gate,
    w_up,
    w_down,
    scale_hidden,
    scale_out,
):
    attended, gate_swapped = attend(queries, keys, values, w_gate[0])
    return experts(
        residual,
        attended,
        norm_gain,
        routes,
        route_weight,
        gate_swapped,
        w_gate[0],
        w_up[0],
        w_down[0],
        scale_hidden[0],
        scale_out,
    )


def solution(mesh):
    in_specs = (
        P(("dp", "context"), "tensor"),
        P(("dp", "context"), "tensor"),
        P(("dp", "context"), "tensor"),
        P(("dp", "context"), "tensor"),
        P("tensor"),
        P(("dp", "context"), None),
        P(("dp", "context"), None),
        P(("dp", "tensor"), None, "context"),
        P(("dp", "tensor"), None, "context"),
        P(("dp", "tensor"), "context", None),
        P(("dp", "tensor"), None, "context"),
        P(("dp", "tensor"), None),
    )
    out_specs = P(("dp", "context"), "tensor")
    return jax.shard_map(local, mesh=mesh, in_specs=in_specs, out_specs=out_specs, check_vma=False)
```

```python
import math

import jax
import jax.numpy as jnp
from jax import lax
from jax.experimental import pallas as pl
from jax.experimental.pallas import tpu as pltpu
from jax.sharding import PartitionSpec as P

D = 4608
HD = 128
EXPERTS = 16
EPS = 1e-06
NEG = -1e30
PIECES = 12
IN_FLIGHT = 2
EARLY = 8
N_CTX = 16
HEADS_HERE = 9
MESH = pl.DeviceIdType.MESH
EXP_SCALE = math.log2(math.e) / math.sqrt(HD)


def head_owner(head, core):
    return lax.rem(lax.div(head * N_CTX, HEADS_HERE) + 8 * core, N_CTX)


def attention_kernel(
    q_ref,
    k_ref,
    v_ref,
    gate_ref,
    out_ref,
    gate_out,
    qs,
    ks,
    vs,
    ob,
    recv_sem,
    send_sem,
    out_send,
    out_recv,
    gate_send,
    gate_recv,
):
    ctx = lax.axis_index("context")
    dp = lax.axis_index("dp")
    core = lax.rem(dp, 2)
    swapping = core != lax.div(ctx, N_CTX // 2)
    diagonal = {"dp": dp + 1 - 2 * core, "context": lax.rem(ctx + N_CTX // 2, N_CTX)}
    rows = q_ref.shape[0]

    barrier = pltpu.get_barrier_semaphore()

    @pl.loop(1, N_CTX)
    def _(step):
        pl.semaphore_signal(
            barrier, inc=1, device_id={"context": lax.rem(ctx + step, N_CTX)}, device_id_type=MESH
        )

    pl.semaphore_signal(barrier, inc=1, device_id=diagonal, device_id_type=MESH)
    pl.semaphore_wait(barrier, N_CTX)
    depth = gate_ref.shape[0] // PIECES

    def piece(number):
        part = pl.ds(pl.multiple_of(number * depth, depth), depth)
        return pltpu.make_async_remote_copy(
            src_ref=gate_ref.at[part, :],
            dst_ref=gate_out.at[part, :],
            send_sem=gate_send.at[number],
            recv_sem=gate_recv,
            device_id=diagonal,
            device_id_type=MESH,
        )

    def pump(first, count):
        @pl.when(swapping)
        def _():
            @pl.loop(first, first + count)
            def _(number):
                piece(number - IN_FLIGHT).wait_send()
                piece(number).start()


    my_rows = pl.ds(pl.multiple_of(ctx * rows, rows), rows)
    sources = (k_ref, q_ref, v_ref)
    targets = (ks, qs, vs)

    def scatter(step, start):
        head = lax.rem(ctx + step, HEADS_HERE)
        owner = head_owner(head, core)
        columns = pl.ds(pl.multiple_of(head * HD, HD), HD)
        for index in range(3):
            src = sources[index].at[:, columns]
            dst = targets[index].at[my_rows, :]

            @pl.when(owner != ctx)
            def _():
                copy = pltpu.make_async_remote_copy(
                    src_ref=src,
                    dst_ref=dst,
                    send_sem=send_sem.at[step, index],
                    recv_sem=recv_sem.at[index],
                    device_id={"context": owner},
                    device_id_type=MESH,
                )
                if start:
                    copy.start()
                else:
                    copy.wait_send()

            if start:

                @pl.when(owner == ctx)
                def _():
                    pltpu.make_async_copy(src, dst, recv_sem.at[index]).start()

    @pl.loop(0, HEADS_HERE)
    def _(step):
        scatter(step, True)

    @pl.when(swapping)
    def _():
        for number in range(IN_FLIGHT):
            piece(number).start()

    base = lax.rem(ctx + 8 * core, N_CTX)
    my_head = lax.div(base * HEADS_HERE + N_CTX - 1, N_CTX)
    active = jnp.logical_and(
        my_head < HEADS_HERE, lax.div(my_head * N_CTX, HEADS_HERE) == base
    )
    head_columns = pl.ds(pl.multiple_of(lax.rem(my_head, HEADS_HERE) * HD, HD), HD)

    def give(block, start):
        src = ob.at[pl.ds(block * rows, rows), :]
        dst = out_ref.at[:, head_columns]

        @pl.when(ctx != block)
        def _():
            copy = pltpu.make_async_remote_copy(
                src_ref=src,
                dst_ref=dst,
                send_sem=out_send.at[block],
                recv_sem=out_recv,
                device_id={"context": block},
                device_id_type=MESH,
            )
            if start:
                copy.start()
            else:
                copy.wait_send()

        if start:

            @pl.when(ctx == block)
            def _():
                pltpu.make_async_copy(src, dst, out_recv).start()

    pump(2, 2)

    @pl.when(active)
    def _():
        for index in range(3):
            pltpu.make_async_copy(targets[index], targets[index], recv_sem.at[index]).wait()
        tile = 2 * rows
        contract = (((1,), (1,)), ((), ()))
        causal = lax.broadcasted_iota(jnp.int32, (tile, tile), 0) >= lax.broadcasted_iota(
            jnp.int32, (tile, tile), 1
        )
        for number in range(N_CTX // 2 - 1, -1, -1):
            low, high = number * tile, (number + 1) * tile
            query = qs[low:high, :]
            own = lax.dot_general(query, ks[low:high, :], contract, preferred_element_type=jnp.float32)
            own = jnp.where(causal, own, NEG)
            top = jnp.max(own, axis=1, keepdims=True)
            if number:
                past = lax.dot_general(
                    query, ks[0:low, :], contract, preferred_element_type=jnp.float32
                )
                top = jnp.maximum(top, jnp.max(past, axis=1, keepdims=True))
            own = jnp.exp2((own - top) * EXP_SCALE)
            total = jnp.sum(own, axis=1, keepdims=True)
            result = jnp.dot(
                own.astype(jnp.bfloat16), vs[low:high, :], preferred_element_type=jnp.float32
            )
            if number:
                past = jnp.exp2((past - top) * EXP_SCALE)
                total = total + jnp.sum(past, axis=1, keepdims=True)
                result = result + jnp.dot(
                    past.astype(jnp.bfloat16), vs[0:low, :], preferred_element_type=jnp.float32
                )
            ob[low:high, :] = (result / total).astype(jnp.bfloat16)
            give(2 * number + 1, True)
            give(2 * number, True)
            if number in (6, 4):
                pump(4 + (6 - number) // 2, 1)
        pump(6, 2)

    @pl.when(jnp.logical_not(active))
    def _():
        pump(4, 4)

    @pl.loop(0, HEADS_HERE)
    def _(step):
        scatter(step, False)

    @pl.when(active)
    def _():
        for block in range(N_CTX):
            give(block, False)

    pltpu.make_async_copy(out_ref, out_ref, out_recv).wait()

    @pl.when(swapping)
    def _():
        for number in range(EARLY - IN_FLIGHT, EARLY):
            piece(number).wait_send()
        landed = gate_out.at[pl.ds(0, EARLY * depth), :]
        pltpu.make_async_copy(landed, landed, gate_recv).wait()


def attend(queries, keys, values, w_gate):
    rows, width = queries.shape
    length = rows * N_CTX
    return pl.pallas_call(
        attention_kernel,
        out_shape=(
            jax.ShapeDtypeStruct((rows, width), jnp.bfloat16),
            jax.ShapeDtypeStruct(w_gate.shape, jnp.bfloat16),
        ),
        in_specs=[pl.BlockSpec(memory_space=pl.ANY)] * 4,
        out_specs=(pl.BlockSpec(memory_space=pltpu.VMEM), pl.BlockSpec(memory_space=pl.ANY)),
        scratch_shapes=[
            pltpu.VMEM((length, HD), jnp.bfloat16),
            pltpu.VMEM((length, HD), jnp.bfloat16),
            pltpu.VMEM((length, HD), jnp.bfloat16),
            pltpu.VMEM((length, HD), jnp.bfloat16),
            pltpu.SemaphoreType.DMA((3,)),
            pltpu.SemaphoreType.DMA((HEADS_HERE, 3)),
            pltpu.SemaphoreType.DMA((N_CTX,)),
            pltpu.SemaphoreType.DMA,
            pltpu.SemaphoreType.DMA((EARLY,)),
            pltpu.SemaphoreType.DMA,
        ],
        compiler_params=pltpu.CompilerParams(
            collective_id=0, has_side_effects=True, vmem_limit_bytes=48 * 1024 * 1024
        ),
        cost_estimate=pl.CostEstimate(
            flops=2 * length * length * HD, bytes_accessed=10**6, transcendentals=length * length // 2
        ),
    )(queries, keys, values, w_gate)


MAIN = 16
TILE_ROWS = 16
SLOT = 64
OVER = 256
GROUP = 16
N_Z = 8
OWN, SIB_OWN = 0, 1


def major(k):
    return 14 if k == 4 else 4 * k - 2


def minor(k):
    return 4 * k - 1


def twin(slot):
    return slot + 1 if slot in (0, 14) else slot + 2


CARRIED = [OWN] + [s for k in (1, 2, 3) for s in (major(k), minor(k))] + [major(4)]
STEPS = [(0, 2), (2, 4), (6, 4), (10, 4), (14, 2)]


def arrived(ref, sem):
    pltpu.make_async_copy(ref, ref, sem).wait()


def one_hot(hit):
    return jnp.where(hit, 1.0, 0.0).astype(jnp.bfloat16)


def exact_dot(left, right):
    return jnp.dot(left, right, preferred_element_type=jnp.float32)


def iotas(rows, columns):
    return (
        lax.broadcasted_iota(jnp.int32, (rows, columns), 0),
        lax.broadcasted_iota(jnp.int32, (rows, columns), 1),
    )


def expert_kernel(
    residual_ref,
    attended_ref,
    gain_ref,
    routes_ref,
    routes_t_ref,
    weight_ref,
    gate_own,
    gate_swapped,
    up_own,
    down_own,
    wide_own,
    tall_own,
    out_ref,
    xm,
    xo,
    ym,
    yo,
    sib_m,
    sib_o,
    rxa_m,
    rxa_o,
    rxb_m,
    rxb_o,
    w1,
    wd,
    wide,
    tall,
    act,
    hid,
    hidden,
    disp_m,
    disp_o,
    eo_m,
    eo_o,
    ret_m,
    ret_o,
    over_x,
    over_y,
    spread,
    gather,
    squares,
    w_recv,
    w_send,
    sq_recv,
    sq_send,
    disp_recv,
    disp_send,
    aga_recv,
    aga_send,
    agb_recv,
    agb_send,
    sibx_recv,
    sibx_send,
    siby_recv,
    siby_send,
    rsa_recv,
    rsa_send,
    rsb_recv,
    rsb_send,
    ret_recv,
    ret_send,
    piece_send,
):
    dp, ctx, tensor = lax.axis_index("dp"), lax.axis_index("context"), lax.axis_index("tensor")
    core, y_hi = lax.rem(dp, 2), lax.div(dp, 2)
    z, y_lo = lax.rem(ctx, N_Z), lax.div(ctx, N_Z)
    sign = 1 - 2 * core
    place = y_hi * 2 + y_lo
    rank = place * 4 + tensor
    rows, quarter = residual_ref.shape
    width = xm.shape[1]
    hid_dev = wd.shape[0]

    def member(number):
        other = lax.div(number, 4)
        return {
            "dp": lax.div(other, 2) * 2 + core,
            "context": lax.rem(other, 2) * N_Z + z,
            "tensor": lax.rem(number, 4),
        }

    ahead = {"context": y_lo * N_Z + lax.rem(z + sign + N_Z, N_Z)}
    behind = {"context": y_lo * N_Z + lax.rem(z - sign + N_Z, N_Z)}
    sibling = {"dp": y_hi * 2 + 1 - core}
    diagonal = {"dp": y_hi * 2 + 1 - core, "context": (1 - y_lo) * N_Z + z}

    barrier = pltpu.get_barrier_semaphore()
    for other in (ahead, behind, sibling, diagonal):
        pl.semaphore_signal(barrier, inc=1, device_id=other, device_id_type=MESH)

    @pl.loop(1, GROUP)
    def _(step):
        pl.semaphore_signal(
            barrier, inc=1, device_id=member(lax.rem(rank + step, GROUP)), device_id_type=MESH
        )

    pl.semaphore_wait(barrier, GROUP + 3)

    pending = []

    def send(src, dst, send_sem, recv_sem, device):
        copy = pltpu.make_async_remote_copy(
            src_ref=src,
            dst_ref=dst,
            send_sem=send_sem,
            recv_sem=recv_sem,
            device_id=device,
            device_id_type=MESH,
        )
        copy.start()
        pending.append(copy)

    swapping = core != y_lo
    up_part = w1.at[:, pl.ds(hid_dev, hid_dev)]
    half_width = width // 2
    early_part = w1.at[pl.ds(0, EARLY * (width // PIECES)), pl.ds(0, hid_dev)]
    late_part = w1.at[pl.ds(EARLY * (width // PIECES), (PIECES - EARLY) * (width // PIECES)), pl.ds(0, hid_dev)]
    down_half = [wd.at[:, pl.ds(half * half_width, half_width)] for half in range(2)]
    moved = (
        (up_own, up_part),
        (down_own.at[:, pl.ds(0, half_width)], down_half[0]),
        (wide_own, wide),
        (tall_own, tall),
        (gate_own.at[pl.ds(0, EARLY * (width // PIECES)), :], early_part),
        (gate_own.at[pl.ds(EARLY * (width // PIECES), (PIECES - EARLY) * (width // PIECES)), :], late_part),
        (down_own.at[:, pl.ds(half_width, half_width)], down_half[1]),
    )

    def swap(index):
        return pltpu.make_async_remote_copy(
            src_ref=moved[index][0],
            dst_ref=moved[index][1],
            send_sem=w_send.at[index],
            recv_sem=w_recv.at[index],
            device_id=diagonal,
            device_id_type=MESH,
        )

    early_rows = EARLY * (width // PIECES)
    n_gate = PIECES - EARLY
    n_pieces = n_gate + 2 * PIECES

    def load(number):
        if number < n_gate + PIECES:
            depth = width // PIECES
            gate_piece = number < n_gate
            start = (EARLY + number if gate_piece else number - n_gate) * depth
            part = pl.ds(start, depth)
            src = (gate_own if gate_piece else up_own).at[part, :]
            dst = w1.at[part, pl.ds(0 if gate_piece else hid_dev, hid_dev)]
            recv_sem = w_recv.at[5 if gate_piece else 0]
        else:
            depth = width // PIECES
            part = pl.ds((number - n_gate - PIECES) * depth, depth)
            src, dst = down_own.at[:, part], wd.at[:, part]
            recv_sem = w_recv.at[1 if number < n_gate + PIECES + PIECES // 2 else 6]
        return pltpu.make_async_remote_copy(
            src_ref=src,
            dst_ref=dst,
            send_sem=piece_send.at[number],
            recv_sem=recv_sem,
            device_id=diagonal,
            device_id_type=MESH,
        )

    progress = [0]

    def pump(count):
        first = progress[0]
        progress[0] = min(first + count, n_pieces)

        @pl.when(swapping)
        def _():
            for number in range(first, progress[0]):
                if number >= IN_FLIGHT:
                    load(number - IN_FLIGHT).wait_send()
                load(number).start()

    @pl.when(swapping)
    def _():
        for index in (2, 3):
            swap(index).start()
        pltpu.make_async_copy(
            gate_swapped.at[pl.ds(0, early_rows), :], early_part, w_recv.at[4]
        ).start()

    @pl.when(jnp.logical_not(swapping))
    def _():
        for index in range(7):
            pltpu.make_async_copy(moved[index][0], moved[index][1], w_recv.at[index]).start()

    pump(IN_FLIGHT)
    state = residual_ref[...].astype(jnp.float32) + attended_ref[...].astype(jnp.float32)
    hidden[...] = state
    own_squares = jnp.sum(state * state, axis=1, keepdims=True)
    squares[tensor] = jnp.broadcast_to(own_squares, (rows, rows)).T[0:8, :]

    def tell(step):
        peer = lax.rem(tensor + step, 4)
        return pltpu.make_async_remote_copy(
            src_ref=squares.at[tensor],
            dst_ref=squares.at[tensor],
            send_sem=sq_send.at[peer],
            recv_sem=sq_recv.at[tensor],
            device_id={"tensor": peer},
            device_id_type=MESH,
        )

    for step in (1, 2, 3):
        tell(step).start()

    row, col = iotas(EXPERTS, rows)
    named = jnp.logical_or(row == routes_t_ref[0:1, :], row == routes_t_ref[1:2, :])
    first, second = iotas(rows, rows)
    ranks = exact_dot(one_hot(named), one_hot(first < second))
    ranks = jnp.where(named, ranks, -1.0)
    row, col = iotas(EXPERTS * MAIN, EXPERTS)
    widened = exact_dot(one_hot((row >> 4) == col), ranks.astype(jnp.bfloat16))
    row, col = iotas(EXPERTS * MAIN, rows)
    pick_main = one_hot(widened == (row & 15).astype(jnp.float32))
    pick_over = one_hot(ranks == float(MAIN))

    for step in (1, 2, 3):
        peer = lax.rem(tensor + step, 4)
        arrived(squares.at[peer], sq_recv.at[peer])
    total = squares[0] + squares[1] + squares[2] + squares[3]
    inverse = lax.rsqrt(total / D + EPS)
    inverse = jnp.broadcast_to(inverse[0:1, :], (rows, rows)).T[:, 0:1]
    normed = (hidden[...] * inverse * gain_ref[...]).astype(jnp.bfloat16)
    disp_m[...] = exact_dot(pick_main, normed).astype(jnp.bfloat16)
    overflow = exact_dot(pick_over, normed).astype(jnp.bfloat16)
    pieces = quarter // HD
    stacked = jnp.concatenate(
        [overflow[:, n * HD : (n + 1) * HD] for n in range(pieces)], axis=0
    )
    row, col = iotas(EXPERTS * TILE_ROWS, EXPERTS * pieces)
    shuffle = one_hot((((col & 15) << 4) | (col >> 4)) == row)
    disp_o[...] = exact_dot(shuffle, stacked).astype(jnp.bfloat16)

    def rows_of(number):
        return pl.ds(pl.multiple_of(number * TILE_ROWS, TILE_ROWS), TILE_ROWS)

    def columns_of(number):
        return pl.ds(pl.multiple_of(number * quarter, quarter), quarter)

    def dispatch(step):
        other = lax.rem(rank + step, GROUP)
        pairs = (
            (disp_m.at[rows_of(other), :], xm.at[rows_of(place), columns_of(tensor)]),
            (disp_o.at[rows_of(other), :], xo.at[rows_of(rank), :]),
        )
        return [
            pltpu.make_async_remote_copy(
                src_ref=src,
                dst_ref=dst,
                send_sem=disp_send.at[step, index],
                recv_sem=disp_recv.at[index],
                device_id=member(other),
                device_id_type=MESH,
            )
            for index, (src, dst) in enumerate(pairs)
        ]

    pltpu.make_async_copy(
        disp_m.at[rows_of(rank), :], xm.at[rows_of(place), columns_of(tensor)], disp_recv.at[0]
    ).start()
    pltpu.make_async_copy(
        disp_o.at[rows_of(rank), :], xo.at[rows_of(rank), :], disp_recv.at[1]
    ).start()

    @pl.loop(1, GROUP)
    def _(step):
        for copy in dispatch(step):
            copy.start()

    row, col = iotas(36 * 16, 4 * OVER)
    chunk, inside = col >> 8, col & 255
    source, part, piece = inside >> 6, (inside >> 4) & 3, inside & 15
    goal = (part * pieces + piece) * 16 + chunk * 4 + source
    spread[...] = one_hot(jnp.logical_and(piece < pieces, goal == row))
    row, col = iotas(4 * OVER, 36 * 16)
    chunk, inside = row >> 8, row & 255
    source, part, piece = inside >> 6, (inside >> 4) & 3, inside & 15
    goal = (part * pieces + piece) * 16 + chunk * 4 + source
    gather[...] = one_hot(jnp.logical_and(piece < pieces, goal == col))

    def main(slot):
        return pl.ds(slot * SLOT, SLOT)

    def over(slot):
        return pl.ds(slot * OVER, OVER)

    def pass_on(slot, goal, send_sem, recv_sem, number, device):
        send(xm.at[main(slot), :], xm.at[main(goal), :], send_sem.at[number, 0], recv_sem.at[number, 0], device)
        send(xo.at[over(slot), :], xo.at[over(goal), :], send_sem.at[number, 1], recv_sem.at[number, 1], device)

    def landed(slot, recv_sem, number):
        arrived(xm.at[main(slot), :], recv_sem.at[number, 0])
        arrived(xo.at[over(slot), :], recv_sem.at[number, 1])

    def share(slot):
        pass_on(slot, twin(slot), sibx_send, sibx_recv, CARRIED.index(slot), sibling)

    pump(3)
    arrived(xm.at[main(OWN), :], disp_recv.at[0])
    arrived(xo.at[over(OWN), :], disp_recv.at[1])
    pass_on(OWN, major(1), aga_send, aga_recv, 0, ahead)
    pass_on(OWN, minor(1), agb_send, agb_recv, 0, behind)
    share(OWN)
    for k in (1, 2, 3):
        pump(4)
        landed(major(k), aga_recv, k - 1)
        pass_on(major(k), major(k + 1), aga_send, aga_recv, k, ahead)
        share(major(k))
        landed(minor(k), agb_recv, k - 1)
        if k < 3:
            pass_on(minor(k), minor(k + 1), agb_send, agb_recv, k, behind)
        share(minor(k))

    def fetch_shared(step):
        low, count = STEPS[step]
        for slot in CARRIED:
            if low <= slot < low + count:
                landed(twin(slot), sibx_recv, CARRIED.index(slot))

    def step_rows(step):
        return STEPS[step][1] * SLOT

    def hidden_part(step):
        low, count = STEPS[step]
        size = step_rows(step)
        tiles = xo[low * OVER : (low + count) * OVER, :]
        stack = exact_dot(spread[:, 0 : count * OVER], tiles).astype(jnp.bfloat16)
        for n in range(36):
            over_x[:, n * HD : (n + 1) * HD] = stack[n * 16 : (n + 1) * 16, :]

        @pl.loop(0, 3)
        def _(n):
            lanes = pl.ds(pl.multiple_of(n * 256, 256), 256)
            rows_in = jnp.concatenate([xm[low * SLOT : low * SLOT + size, :], over_x[...]], axis=0)
            hid[0 : size + 16, lanes] = exact_dot(rows_in, w1[:, lanes])

        for n in range(hid_dev // HD):
            lanes = slice(n * HD, (n + 1) * HD)
            gate = hid[0 : size + 16, lanes] * tall[n : n + 1, :]
            up = hid[0 : size + 16, hid_dev + n * HD : hid_dev + (n + 1) * HD] * tall[n + 3 : n + 4, :]
            act[step * 272 : step * 272 + size + 16, lanes] = (
                gate / (1.0 + jnp.exp(-gate)) * up
            ).astype(jnp.bfloat16)

    def lanes_of(half, n):
        start = half * half_width + n * 768
        return pl.ds(start if isinstance(n, int) else pl.multiple_of(start, 256), 768)

    def down_part(step, half):
        low, count = STEPS[step]
        size = step_rows(step)

        @pl.loop(0, half_width // 768)
        def _(n):
            lanes = lanes_of(half, n)
            result = exact_dot(act[step * 272 : step * 272 + size + 16, :], wd[:, lanes])
            result = result.astype(jnp.bfloat16)
            ym[low * SLOT : low * SLOT + size, lanes] = result[0:size, :]
            over_y[step * 16 : step * 16 + 16, lanes] = result[size:, :]

        if half:
            stack = jnp.concatenate(
                [over_y[step * 16 : step * 16 + 16, n * HD : (n + 1) * HD] for n in range(36)], axis=0
            )
            yo[low * OVER : (low + count) * OVER, :] = exact_dot(
                gather[0 : count * OVER, :], stack
            ).astype(jnp.bfloat16)
        part = pl.ds(half * half_width, half_width)
        for slot in CARRIED:
            if low <= slot < low + count:
                number = CARRIED.index(slot)
                other = twin(slot)
                send(
                    ym.at[main(other), part],
                    sib_m.at[number, :, part],
                    siby_send.at[number, half],
                    siby_recv.at[number, half],
                    sibling,
                )
                if half:
                    send(
                        yo.at[over(other), :],
                        sib_o.at[number],
                        siby_send.at[number, 2],
                        siby_recv.at[number, 2],
                        sibling,
                    )

    pump(3)
    arrived(early_part, w_recv.at[4])
    arrived(late_part, w_recv.at[5])
    arrived(up_part, w_recv.at[0])
    arrived(wide, w_recv.at[2])
    arrived(tall, w_recv.at[3])
    for step in (0, 1, 2, 3):
        fetch_shared(step)
        hidden_part(step)
        pump(1)
    landed(major(4), aga_recv, 3)
    share(major(4))
    fetch_shared(4)
    hidden_part(4)
    pump(max(0, n_gate + PIECES + PIECES // 2 - progress[0]))
    arrived(down_half[0], w_recv.at[1])

    def summed(own, others):
        value = own.astype(jnp.float32)
        for other in others:
            value = value + other.astype(jnp.float32)
        return value

    def await_parts(slot, extras, half):
        number = CARRIED.index(slot)
        part = pl.ds(half * half_width, half_width)
        arrived(sib_m.at[number, :, part], siby_recv.at[number, half])
        for ref_m, ref_o, spot, sems in extras:
            arrived(ref_m.at[spot, :, part], sems.at[spot, half])
        if half:
            arrived(sib_o.at[number], siby_recv.at[number, 2])
            for ref_m, ref_o, spot, sems in extras:
                arrived(ref_o.at[spot], sems.at[spot, 2])

    def block(slot, extras, lanes):
        number = CARRIED.index(slot)
        return summed(
            ym[main(slot), lanes],
            [sib_m[number, :, lanes]] + [extra[0][extra[2], :, lanes] for extra in extras],
        )

    def tiles(slot, extras):
        number = CARRIED.index(slot)
        return summed(yo[over(slot), :], [sib_o[number]] + [extra[1][extra[2]] for extra in extras])

    def hop(slot, extras, half, goal_m, goal_o, send_sem, recv_sem, number, device):
        await_parts(slot, extras, half)

        @pl.loop(0, half_width // 768)
        def _(n):
            lanes = lanes_of(half, n)
            ym[main(slot), lanes] = block(slot, extras, lanes).astype(jnp.bfloat16)

        part = pl.ds(half * half_width, half_width)
        send(
            ym.at[main(slot), part],
            goal_m.at[number, :, part],
            send_sem.at[number, half],
            recv_sem.at[number, half],
            device,
        )
        if half:
            yo[over(slot), :] = tiles(slot, extras).astype(jnp.bfloat16)
            send(
                yo.at[over(slot), :],
                goal_o.at[number],
                send_sem.at[number, 2],
                recv_sem.at[number, 2],
                device,
            )

    def hop_a(k, half):
        extras = [(rxa_m, rxa_o, k, rsa_recv)] if k < 4 else []
        hop(major(k), extras, half, rxa_m, rxa_o, rsa_send, rsa_recv, k - 1, behind)

    def hop_b(k, half):
        extras = [(rxb_m, rxb_o, k, rsb_recv)] if k < 3 else []
        hop(minor(k), extras, half, rxb_m, rxb_o, rsb_send, rsb_recv, k - 1, ahead)

    def give_back(step, half):
        spot = lax.rem(place + lax.div(step, 2), 4)
        part = 2 * half + lax.rem(tensor + step, 2)
        other = spot * 4 + part
        return other, eo_m.at[rows_of(spot), columns_of(part)], ret_m.at[rows_of(rank), :]

    def give_all(half, start):
        @pl.loop(0, 8)
        def _(step):
            other, src, dst = give_back(step, half)

            @pl.when(other != rank)
            def _():
                copy = pltpu.make_async_remote_copy(
                    src_ref=src,
                    dst_ref=dst,
                    send_sem=ret_send.at[half * 8 + step, 0],
                    recv_sem=ret_recv.at[0],
                    device_id=member(other),
                    device_id_type=MESH,
                )
                if start:
                    copy.start()
                else:
                    copy.wait_send()

            if start:

                @pl.when(other == rank)
                def _():
                    pltpu.make_async_copy(src, dst, ret_recv.at[0]).start()

    def give_over(step):
        other = lax.rem(rank + step, GROUP)
        return pltpu.make_async_remote_copy(
            src_ref=eo_o.at[rows_of(other), :],
            dst_ref=ret_o.at[rows_of(rank), :],
            send_sem=ret_send.at[step, 1],
            recv_sem=ret_recv.at[1],
            device_id=member(other),
            device_id_type=MESH,
        )

    def finish(half):
        last = [(rxb_m, rxb_o, 0, rsb_recv), (rxa_m, rxa_o, 0, rsa_recv)]
        await_parts(OWN, last, half)

        @pl.loop(0, half_width // 768)
        def _(n):
            lanes = lanes_of(half, n)
            eo_m[:, lanes] = (block(OWN, last, lanes) * wide[0:1, lanes]).astype(jnp.bfloat16)

        if half:
            value = tiles(OWN, last)
            for n in range(4):
                eo_o[n * 64 : (n + 1) * 64, :] = (
                    value[n * 64 : (n + 1) * 64, :] * tall[8:72, :]
                ).astype(jnp.bfloat16)
        give_all(half, True)
        if half:
            pltpu.make_async_copy(
                eo_o.at[rows_of(rank), :], ret_o.at[rows_of(rank), :], ret_recv.at[1]
            ).start()

            @pl.loop(1, GROUP)
            def _(step):
                give_over(step).start()

    down_part(4, 0)
    hop_a(4, 0)
    down_part(3, 0)
    hop_b(3, 0)
    for step in (2, 1, 0):
        pump(1)
        down_part(step, 0)
    hop_a(3, 0)
    hop_b(2, 0)
    pump(1)
    hop_a(2, 0)
    hop_b(1, 0)
    pump(n_pieces)
    arrived(down_half[1], w_recv.at[6])
    down_part(4, 1)
    hop_a(4, 1)
    down_part(3, 1)
    hop_b(3, 1)
    hop_a(1, 0)
    down_part(2, 1)
    hop_a(3, 1)
    hop_b(2, 1)
    down_part(1, 1)
    hop_a(2, 1)
    hop_b(1, 1)
    down_part(0, 1)
    finish(0)
    hop_a(1, 1)
    finish(1)

    expert_id = iotas(rows, EXPERTS)[1]
    hits = [expert_id == routes_ref[:, k : k + 1] for k in range(2)]
    first, second = iotas(rows, rows)
    both = one_hot(jnp.logical_or(hits[0], hits[1]))
    token_ranks = exact_dot(one_hot(second < first), both)
    row, col = iotas(EXPERTS, EXPERTS * MAIN)
    expand = one_hot((col >> 4) == row)
    slot_rank = (iotas(rows, EXPERTS * MAIN)[1] & 15).astype(jnp.float32)
    selects = []
    for k in range(2):
        own_ranks = jnp.where(hits[k], token_ranks, -1.0)
        wide_ranks = exact_dot(own_ranks.astype(jnp.bfloat16), expand)
        selects.append((one_hot(wide_ranks == slot_rank), one_hot(own_ranks == float(MAIN))))
    row, col = iotas(EXPERTS * pieces, EXPERTS * TILE_ROWS)
    unshuffle = one_hot((((row & 15) << 4) | (row >> 4)) == col)

    arrived(ret_m, ret_recv.at[0])
    arrived(ret_o, ret_recv.at[1])
    back = exact_dot(unshuffle, ret_o[...]).astype(jnp.bfloat16)
    back = jnp.concatenate(
        [back[n * EXPERTS : (n + 1) * EXPERTS, :] for n in range(pieces)], axis=1
    )
    routed = jnp.zeros((rows, quarter), jnp.float32)
    for k in range(2):
        picked = exact_dot(selects[k][0], ret_m[...]) + exact_dot(selects[k][1], back)
        routed = routed + picked * weight_ref[:, k : k + 1]
    out_ref[...] = (hidden[...] + routed).astype(jnp.bfloat16)

    for copy in pending:
        copy.wait_send()
    for step in (1, 2, 3):
        tell(step).wait_send()

    @pl.loop(1, GROUP)
    def _(step):
        for copy in dispatch(step) + [give_over(step)]:
            copy.wait_send()

    for half in range(2):
        give_all(half, False)

    @pl.when(swapping)
    def _():
        for index in (2, 3):
            swap(index).wait_send()
        for number in range(n_pieces - IN_FLIGHT, n_pieces):
            load(number).wait_send()


def experts(
    residual, attended, norm_gain, routes, route_weight, gate_swapped, w_gate, w_up, w_down, scale_hidden, scale_out
):
    rows, quarter = residual.shape
    width, hid_dev = w_gate.shape
    wide = jnp.broadcast_to(scale_out, (8, width))
    pieces = quarter // HD
    tall = jnp.concatenate(
        [
            jnp.pad(scale_hidden.reshape(2 * hid_dev // HD, HD), ((0, 2), (0, 0))),
            jnp.pad(scale_out.reshape(4, pieces, HD), ((0, 0), (0, 16 - pieces), (0, 0))).reshape(64, HD),
        ],
        axis=0,
    )
    vmem = pl.BlockSpec(memory_space=pltpu.VMEM)
    hbm = pl.BlockSpec(memory_space=pl.ANY)
    half = jnp.bfloat16
    dma = pltpu.SemaphoreType.DMA
    return pl.pallas_call(
        expert_kernel,
        out_shape=jax.ShapeDtypeStruct((rows, quarter), half),
        in_specs=[vmem] * 6 + [hbm] * 6,
        out_specs=vmem,
        scratch_shapes=[
            pltpu.VMEM((16 * SLOT, width), half),
            pltpu.VMEM((16 * OVER, HD), half),
            pltpu.VMEM((16 * SLOT, width), half),
            pltpu.VMEM((16 * OVER, HD), half),
            pltpu.VMEM((8, SLOT, width), half),
            pltpu.VMEM((8, OVER, HD), half),
            pltpu.VMEM((4, SLOT, width), half),
            pltpu.VMEM((4, OVER, HD), half),
            pltpu.VMEM((3, SLOT, width), half),
            pltpu.VMEM((3, OVER, HD), half),
            pltpu.VMEM((width, 2 * hid_dev), half),
            pltpu.VMEM((hid_dev, width), half),
            pltpu.VMEM((8, width), jnp.float32),
            pltpu.VMEM((72, HD), jnp.float32),
            pltpu.VMEM((5 * 272, hid_dev), half),
            pltpu.VMEM((272, 2 * hid_dev), jnp.float32),
            pltpu.VMEM((rows, quarter), jnp.float32),
            pltpu.VMEM((EXPERTS * MAIN, quarter), half),
            pltpu.VMEM((EXPERTS * TILE_ROWS, HD), half),
            pltpu.VMEM((SLOT, width), half),
            pltpu.VMEM((OVER, HD), half),
            pltpu.VMEM((EXPERTS * MAIN, quarter), half),
            pltpu.VMEM((EXPERTS * TILE_ROWS, HD), half),
            pltpu.VMEM((16, width), half),
            pltpu.VMEM((80, width), half),
            pltpu.VMEM((36 * 16, 4 * OVER), half),
            pltpu.VMEM((4 * OVER, 36 * 16), half),
            pltpu.VMEM((4, 8, rows), jnp.float32),
            dma((7,)),
            dma((4,)),
            dma((4,)),
            dma((4,)),
            dma((2,)),
            dma((GROUP, 2)),
            dma((4, 2)),
            dma((4, 2)),
            dma((3, 2)),
            dma((3, 2)),
            dma((8, 2)),
            dma((8, 2)),
            dma((8, 3)),
            dma((8, 3)),
            dma((4, 3)),
            dma((4, 3)),
            dma((3, 3)),
            dma((3, 3)),
            dma((2,)),
            dma((GROUP, 2)),
            dma((3 * PIECES - EARLY,)),
        ],
        compiler_params=pltpu.CompilerParams(
            collective_id=1, has_side_effects=True, vmem_limit_bytes=60 * 1024 * 1024
        ),
        cost_estimate=pl.CostEstimate(
            flops=6 * 1088 * width * hid_dev, bytes_accessed=12 * 10**6, transcendentals=10**6
        ),
    )(
        residual,
        attended,
        norm_gain.reshape(1, quarter),
        routes,
        routes.T,
        route_weight,
        w_gate,
        gate_swapped,
        w_up,
        w_down,
        wide,
        tall,
    )


def local(
    queries,
    keys,
    values,
    residual,
    norm_gain,
    routes,
    route_weight,
    w_gate,
    w_up,
    w_down,
    scale_hidden,
    scale_out,
):
    attended, gate_swapped = attend(queries, keys, values, w_gate[0])
    return experts(
        residual,
        attended,
        norm_gain,
        routes,
        route_weight,
        gate_swapped,
        w_gate[0],
        w_up[0],
        w_down[0],
        scale_hidden[0],
        scale_out,
    )


def solution(mesh):
    in_specs = (
        P(("dp", "context"), "tensor"),
        P(("dp", "context"), "tensor"),
        P(("dp", "context"), "tensor"),
        P(("dp", "context"), "tensor"),
        P("tensor"),
        P(("dp", "context"), None),
        P(("dp", "context"), None),
        P(("dp", "tensor"), None, "context"),
        P(("dp", "tensor"), None, "context"),
        P(("dp", "tensor"), "context", None),
        P(("dp", "tensor"), None, "context"),
        P(("dp", "tensor"), None),
    )
    out_specs = P(("dp", "context"), "tensor")
    return jax.shard_map(local, mesh=mesh, in_specs=in_specs, out_specs=out_specs, check_vma=False)
```

```python
import math

import jax
import jax.numpy as jnp
from jax import lax
from jax.experimental import pallas as pl
from jax.experimental.pallas import tpu as pltpu
from jax.sharding import PartitionSpec as P

D = 4608
HD = 128
EXPERTS = 16
EPS = 1e-06
NEG = -1e30
PIECES = 12
IN_FLIGHT = 3
EARLY = 12
N_CTX = 16
HEADS_HERE = 9
MESH = pl.DeviceIdType.MESH
EXP_SCALE = math.log2(math.e) / math.sqrt(HD)


def head_owner(head, core):
    return lax.rem(lax.div(head * N_CTX, HEADS_HERE) + 8 * core, N_CTX)


def attention_phase(
    q_ref, k_ref, v_ref, out_ref, qs, ks, vs, ob, recv_sem, send_sem, out_send, out_recv, pump
):
    ctx = lax.axis_index("context")
    core = lax.rem(lax.axis_index("dp"), 2)
    rows = q_ref.shape[0]
    my_rows = pl.ds(pl.multiple_of(ctx * rows, rows), rows)
    sources = (k_ref, q_ref, v_ref)
    targets = (ks, qs, vs)

    def scatter(step, start):
        head = lax.rem(ctx + step, HEADS_HERE)
        owner = head_owner(head, core)
        columns = pl.ds(pl.multiple_of(head * HD, HD), HD)
        for index in range(3):
            src = sources[index].at[:, columns]
            dst = targets[index].at[my_rows, :]

            @pl.when(owner != ctx)
            def _():
                copy = pltpu.make_async_remote_copy(
                    src_ref=src,
                    dst_ref=dst,
                    send_sem=send_sem.at[step, index],
                    recv_sem=recv_sem.at[index],
                    device_id={"context": owner},
                    device_id_type=MESH,
                )
                if start:
                    copy.start()
                else:
                    copy.wait_send()

            if start:

                @pl.when(owner == ctx)
                def _():
                    pltpu.make_async_copy(src, dst, recv_sem.at[index]).start()

    @pl.loop(0, HEADS_HERE)
    def _(step):
        scatter(step, True)

    pump(0, 4)

    base = lax.rem(ctx + 8 * core, N_CTX)
    my_head = lax.div(base * HEADS_HERE + N_CTX - 1, N_CTX)
    active = jnp.logical_and(
        my_head < HEADS_HERE, lax.div(my_head * N_CTX, HEADS_HERE) == base
    )
    head_columns = pl.ds(pl.multiple_of(lax.rem(my_head, HEADS_HERE) * HD, HD), HD)

    def give(block, start):
        src = ob.at[pl.ds(block * rows, rows), :]
        dst = out_ref.at[:, head_columns]

        @pl.when(ctx != block)
        def _():
            copy = pltpu.make_async_remote_copy(
                src_ref=src,
                dst_ref=dst,
                send_sem=out_send.at[block],
                recv_sem=out_recv,
                device_id={"context": block},
                device_id_type=MESH,
            )
            if start:
                copy.start()
            else:
                copy.wait_send()

        if start:

            @pl.when(ctx == block)
            def _():
                pltpu.make_async_copy(src, dst, out_recv).start()

    @pl.when(active)
    def _():
        for index in range(3):
            pltpu.make_async_copy(targets[index], targets[index], recv_sem.at[index]).wait()
        tile = 2 * rows
        contract = (((1,), (1,)), ((), ()))
        causal = lax.broadcasted_iota(jnp.int32, (tile, tile), 0) >= lax.broadcasted_iota(
            jnp.int32, (tile, tile), 1
        )
        for number in range(N_CTX // 2 - 1, -1, -1):
            low, high = number * tile, (number + 1) * tile
            query = qs[low:high, :]
            own = lax.dot_general(query, ks[low:high, :], contract, preferred_element_type=jnp.float32)
            own = jnp.where(causal, own, NEG)
            top = jnp.max(own, axis=1, keepdims=True)
            if number:
                past = lax.dot_general(
                    query, ks[0:low, :], contract, preferred_element_type=jnp.float32
                )
                top = jnp.maximum(top, jnp.max(past, axis=1, keepdims=True))
            own = jnp.exp2((own - top) * EXP_SCALE)
            total = jnp.sum(own, axis=1, keepdims=True)
            result = jnp.dot(
                own.astype(jnp.bfloat16), vs[low:high, :], preferred_element_type=jnp.float32
            )
            if number:
                past = jnp.exp2((past - top) * EXP_SCALE)
                total = total + jnp.sum(past, axis=1, keepdims=True)
                result = result + jnp.dot(
                    past.astype(jnp.bfloat16), vs[0:low, :], preferred_element_type=jnp.float32
                )
            ob[low:high, :] = (result / total).astype(jnp.bfloat16)
            give(2 * number + 1, True)
            give(2 * number, True)
            if number in (6, 4):
                pump(4 + (6 - number) // 2, 1)
        pump(6, EARLY - 6)

    @pl.when(jnp.logical_not(active))
    def _():
        pump(4, EARLY - 4)

    @pl.loop(0, HEADS_HERE)
    def _(step):
        scatter(step, False)

    @pl.when(active)
    def _():
        for block in range(N_CTX):
            give(block, False)

    pltpu.make_async_copy(out_ref, out_ref, out_recv).wait()


MAIN = 16
TILE_ROWS = 16
SLOT = 64
OVER = 256
GROUP = 16
N_Z = 8
OWN, SIB_OWN = 0, 1


def major(k):
    return 14 if k == 4 else 4 * k - 2


def minor(k):
    return 4 * k - 1


def twin(slot):
    return slot + 1 if slot in (0, 14) else slot + 2


CARRIED = [OWN] + [s for k in (1, 2, 3) for s in (major(k), minor(k))] + [major(4)]
STEPS = [(0, 2), (2, 4), (6, 4), (10, 4), (14, 2)]


def arrived(ref, sem):
    pltpu.make_async_copy(ref, ref, sem).wait()


def one_hot(hit):
    return jnp.where(hit, 1.0, 0.0).astype(jnp.bfloat16)


def exact_dot(left, right):
    return jnp.dot(left, right, preferred_element_type=jnp.float32)


def iotas(rows, columns):
    return (
        lax.broadcasted_iota(jnp.int32, (rows, columns), 0),
        lax.broadcasted_iota(jnp.int32, (rows, columns), 1),
    )


def layer_kernel(
    gain_ref,
    routes_ref,
    weight_ref,
    residual_ref,
    q_ref,
    k_ref,
    v_ref,
    gate_all,
    up_all,
    down_all,
    inner_all,
    wide_own,
    out_ref,
    residual,
    attended,
    qs,
    ks,
    vs,
    ob,
    xm,
    xo,
    ym,
    yo,
    sib_m,
    sib_o,
    rxa_m,
    rxa_o,
    rxb_m,
    rxb_o,
    w1,
    wd,
    wide,
    inner,
    tall,
    act,
    hid,
    hidden,
    disp_m,
    disp_o,
    eo_m,
    eo_o,
    ret_m,
    ret_o,
    over_x,
    over_y,
    spread,
    gather,
    squares,
    w_recv,
    w_send,
    sq_recv,
    sq_send,
    disp_recv,
    disp_send,
    aga_recv,
    aga_send,
    agb_recv,
    agb_send,
    sibx_recv,
    sibx_send,
    siby_recv,
    siby_send,
    rsa_recv,
    rsa_send,
    rsb_recv,
    rsb_send,
    ret_recv,
    ret_send,
    piece_send,
    attn_recv,
    attn_send,
    out_send,
    out_recv,
    res_recv,
):
    dp, ctx, tensor = lax.axis_index("dp"), lax.axis_index("context"), lax.axis_index("tensor")
    core, y_hi = lax.rem(dp, 2), lax.div(dp, 2)
    z, y_lo = lax.rem(ctx, N_Z), lax.div(ctx, N_Z)
    sign = 1 - 2 * core
    place = y_hi * 2 + y_lo
    rank = place * 4 + tensor
    rows, quarter = residual_ref.shape
    width = xm.shape[1]
    hid_dev = wd.shape[0]
    gate_own, up_own, down_own, inner_own = (
        ref.at[0] for ref in (gate_all, up_all, down_all, inner_all)
    )

    def member(number):
        other = lax.div(number, 4)
        return {
            "dp": lax.div(other, 2) * 2 + core,
            "context": lax.rem(other, 2) * N_Z + z,
            "tensor": lax.rem(number, 4),
        }

    ahead = {"context": y_lo * N_Z + lax.rem(z + sign + N_Z, N_Z)}
    behind = {"context": y_lo * N_Z + lax.rem(z - sign + N_Z, N_Z)}
    sibling = {"dp": y_hi * 2 + 1 - core}
    diagonal = {"dp": y_hi * 2 + 1 - core, "context": (1 - y_lo) * N_Z + z}

    barrier = pltpu.get_barrier_semaphore()
    for other in (ahead, behind, sibling, diagonal):
        pl.semaphore_signal(barrier, inc=1, device_id=other, device_id_type=MESH)

    @pl.loop(1, GROUP)
    def _(step):
        pl.semaphore_signal(
            barrier, inc=1, device_id=member(lax.rem(rank + step, GROUP)), device_id_type=MESH
        )

    @pl.loop(1, N_CTX)
    def _(step):
        pl.semaphore_signal(
            barrier, inc=1, device_id={"context": lax.rem(ctx + step, N_CTX)}, device_id_type=MESH
        )

    load_residual = pltpu.make_async_copy(residual_ref, residual, res_recv)
    load_residual.start()
    pl.semaphore_wait(barrier, GROUP + N_CTX + 2)

    pending = []

    def send(src, dst, send_sem, recv_sem, device):
        copy = pltpu.make_async_remote_copy(
            src_ref=src,
            dst_ref=dst,
            send_sem=send_sem,
            recv_sem=recv_sem,
            device_id=device,
            device_id_type=MESH,
        )
        copy.start()
        pending.append(copy)

    swapping = core != y_lo
    gate_part = w1.at[:, pl.ds(0, hid_dev)]
    up_part = w1.at[:, pl.ds(hid_dev, hid_dev)]
    half_width = width // 2
    down_half = [wd.at[:, pl.ds(half * half_width, half_width)] for half in range(2)]
    moved = (
        (gate_own, gate_part),
        (up_own, up_part),
        (down_own.at[:, pl.ds(0, half_width)], down_half[0]),
        (down_own.at[:, pl.ds(half_width, half_width)], down_half[1]),
        (inner_own, inner),
        (wide_own, wide),
    )

    def swap(index):
        return pltpu.make_async_remote_copy(
            src_ref=moved[index][0],
            dst_ref=moved[index][1],
            send_sem=w_send.at[index],
            recv_sem=w_recv.at[index],
            device_id=diagonal,
            device_id_type=MESH,
        )

    n_pieces = 3 * PIECES
    depth = width // PIECES

    def load(number):
        which, part = number // PIECES, pl.ds(number % PIECES * depth, depth)
        if which < 2:
            src = (gate_own, up_own)[which].at[part, :]
            dst = w1.at[part, pl.ds(which * hid_dev, hid_dev)]
        else:
            src, dst = down_own.at[:, part], wd.at[:, part]
            which += number % PIECES // (PIECES // 2)
        return pltpu.make_async_remote_copy(
            src_ref=src,
            dst_ref=dst,
            send_sem=piece_send.at[number],
            recv_sem=w_recv.at[which],
            device_id=diagonal,
            device_id_type=MESH,
        )

    def pump_at(first, count):
        @pl.when(swapping)
        def _():
            for number in range(first, first + count):
                if number >= IN_FLIGHT:
                    load(number - IN_FLIGHT).wait_send()
                load(number).start()

    progress = [EARLY]

    def pump(count):
        first = progress[0]
        progress[0] = min(first + max(count, 0), n_pieces)
        if progress[0] > first:
            pump_at(first, progress[0] - first)

    @pl.when(swapping)
    def _():
        for index in (4, 5):
            swap(index).start()

    @pl.when(jnp.logical_not(swapping))
    def _():
        for index in range(6):
            pltpu.make_async_copy(moved[index][0], moved[index][1], w_recv.at[index]).start()

    attention_phase(
        q_ref, k_ref, v_ref, attended, qs, ks, vs, ob, attn_recv, attn_send, out_send, out_recv, pump_at
    )
    load_residual.wait()

    def upright(line):
        return jnp.broadcast_to(line, (rows, rows)).T[:, 0:1]

    state = residual[...].astype(jnp.float32) + attended[...].astype(jnp.float32)
    hidden[...] = state
    own_squares = jnp.sum(state * state, axis=1, keepdims=True)
    squares[tensor] = jnp.broadcast_to(own_squares, (rows, rows)).T[0:8, :]

    def tell(step):
        peer = lax.rem(tensor + step, 4)
        return pltpu.make_async_remote_copy(
            src_ref=squares.at[tensor],
            dst_ref=squares.at[tensor],
            send_sem=sq_send.at[peer],
            recv_sem=sq_recv.at[tensor],
            device_id={"tensor": peer},
            device_id_type=MESH,
        )

    for step in (1, 2, 3):
        tell(step).start()

    pump(1)
    row, col = iotas(EXPERTS, rows)
    named = jnp.logical_or(row == routes_ref[0:1, :], row == routes_ref[1:2, :])
    first, second = iotas(rows, rows)
    ranks = exact_dot(one_hot(named), one_hot(first < second))
    ranks = jnp.where(named, ranks, -1.0)
    row, col = iotas(EXPERTS * MAIN, EXPERTS)
    widened = exact_dot(one_hot((row >> 4) == col), ranks.astype(jnp.bfloat16))
    row, col = iotas(EXPERTS * MAIN, rows)
    pick_main = one_hot(widened == (row & 15).astype(jnp.float32))
    pick_over = one_hot(ranks == float(MAIN))

    for step in (1, 2, 3):
        peer = lax.rem(tensor + step, 4)
        arrived(squares.at[peer], sq_recv.at[peer])
    total = squares[0] + squares[1] + squares[2] + squares[3]
    inverse = lax.rsqrt(total / D + EPS)
    normed = (hidden[...] * upright(inverse[0:1, :]) * gain_ref[...]).astype(jnp.bfloat16)
    disp_m[...] = exact_dot(pick_main, normed).astype(jnp.bfloat16)
    overflow = exact_dot(pick_over, normed).astype(jnp.bfloat16)
    pieces = quarter // HD
    stacked = jnp.concatenate(
        [overflow[:, n * HD : (n + 1) * HD] for n in range(pieces)], axis=0
    )
    row, col = iotas(EXPERTS * TILE_ROWS, EXPERTS * pieces)
    shuffle = one_hot((((col & 15) << 4) | (col >> 4)) == row)
    disp_o[...] = exact_dot(shuffle, stacked).astype(jnp.bfloat16)

    def rows_of(number):
        return pl.ds(pl.multiple_of(number * TILE_ROWS, TILE_ROWS), TILE_ROWS)

    def columns_of(number):
        return pl.ds(pl.multiple_of(number * quarter, quarter), quarter)

    def dispatch(step):
        other = lax.rem(rank + step, GROUP)
        pairs = (
            (disp_m.at[rows_of(other), :], xm.at[rows_of(place), columns_of(tensor)]),
            (disp_o.at[rows_of(other), :], xo.at[rows_of(rank), :]),
        )
        return [
            pltpu.make_async_remote_copy(
                src_ref=src,
                dst_ref=dst,
                send_sem=disp_send.at[step, index],
                recv_sem=disp_recv.at[index],
                device_id=member(other),
                device_id_type=MESH,
            )
            for index, (src, dst) in enumerate(pairs)
        ]

    pltpu.make_async_copy(
        disp_m.at[rows_of(rank), :], xm.at[rows_of(place), columns_of(tensor)], disp_recv.at[0]
    ).start()
    pltpu.make_async_copy(
        disp_o.at[rows_of(rank), :], xo.at[rows_of(rank), :], disp_recv.at[1]
    ).start()

    @pl.loop(1, GROUP)
    def _(step):
        for copy in dispatch(step):
            copy.start()

    row, col = iotas(36 * 16, 4 * OVER)
    chunk, inside = col >> 8, col & 255
    source, part, piece = inside >> 6, (inside >> 4) & 3, inside & 15
    goal = (part * pieces + piece) * 16 + chunk * 4 + source
    spread[...] = one_hot(jnp.logical_and(piece < pieces, goal == row))
    row, col = iotas(4 * OVER, 36 * 16)
    chunk, inside = row >> 8, row & 255
    source, part, piece = inside >> 6, (inside >> 4) & 3, inside & 15
    goal = (part * pieces + piece) * 16 + chunk * 4 + source
    gather[...] = one_hot(jnp.logical_and(piece < pieces, goal == col))

    def main(slot):
        return pl.ds(slot * SLOT, SLOT)

    def over(slot):
        return pl.ds(slot * OVER, OVER)

    def pass_on(slot, goal, send_sem, recv_sem, number, device):
        send(xm.at[main(slot), :], xm.at[main(goal), :], send_sem.at[number, 0], recv_sem.at[number, 0], device)
        send(xo.at[over(slot), :], xo.at[over(goal), :], send_sem.at[number, 1], recv_sem.at[number, 1], device)

    def landed(slot, recv_sem, number):
        arrived(xm.at[main(slot), :], recv_sem.at[number, 0])
        arrived(xo.at[over(slot), :], recv_sem.at[number, 1])

    def share(slot):
        pass_on(slot, twin(slot), sibx_send, sibx_recv, CARRIED.index(slot), sibling)

    pump(3)
    arrived(xm.at[main(OWN), :], disp_recv.at[0])
    arrived(xo.at[over(OWN), :], disp_recv.at[1])
    pass_on(OWN, major(1), aga_send, aga_recv, 0, ahead)
    pass_on(OWN, minor(1), agb_send, agb_recv, 0, behind)
    share(OWN)
    for k in (1, 2, 3):
        pump(4)
        landed(major(k), aga_recv, k - 1)
        pass_on(major(k), major(k + 1), aga_send, aga_recv, k, ahead)
        share(major(k))
        landed(minor(k), agb_recv, k - 1)
        if k < 3:
            pass_on(minor(k), minor(k + 1), agb_send, agb_recv, k, behind)
        share(minor(k))

    def fetch_shared(step):
        low, count = STEPS[step]
        for slot in CARRIED:
            if low <= slot < low + count:
                landed(twin(slot), sibx_recv, CARRIED.index(slot))

    def step_rows(step):
        return STEPS[step][1] * SLOT

    def hidden_part(step):
        low, count = STEPS[step]
        size = step_rows(step)
        tiles = xo[low * OVER : (low + count) * OVER, :]
        stack = exact_dot(spread[:, 0 : count * OVER], tiles).astype(jnp.bfloat16)
        for n in range(36):
            over_x[:, n * HD : (n + 1) * HD] = stack[n * 16 : (n + 1) * 16, :]

        @pl.loop(0, 3)
        def _(n):
            lanes = pl.ds(pl.multiple_of(n * 256, 256), 256)
            rows_in = jnp.concatenate([xm[low * SLOT : low * SLOT + size, :], over_x[...]], axis=0)
            hid[0 : size + 16, lanes] = exact_dot(rows_in, w1[:, lanes])

        for n in range(hid_dev // HD):
            lanes = slice(n * HD, (n + 1) * HD)
            gate = hid[0 : size + 16, lanes] * inner[0:1, lanes]
            up = hid[0 : size + 16, hid_dev + n * HD : hid_dev + (n + 1) * HD] * inner[1:2, lanes]
            act[step * 272 : step * 272 + size + 16, lanes] = (
                gate / (1.0 + jnp.exp(-gate)) * up
            ).astype(jnp.bfloat16)

    def lanes_of(half, n):
        start = half * half_width + n * 768
        return pl.ds(start if isinstance(n, int) else pl.multiple_of(start, 256), 768)

    def down_part(step, half):
        low, count = STEPS[step]
        size = step_rows(step)

        @pl.loop(0, half_width // 768)
        def _(n):
            lanes = lanes_of(half, n)
            result = exact_dot(act[step * 272 : step * 272 + size + 16, :], wd[:, lanes])
            result = result.astype(jnp.bfloat16)
            ym[low * SLOT : low * SLOT + size, lanes] = result[0:size, :]
            over_y[step * 16 : step * 16 + 16, lanes] = result[size:, :]

        if half:
            stack = jnp.concatenate(
                [over_y[step * 16 : step * 16 + 16, n * HD : (n + 1) * HD] for n in range(36)], axis=0
            )
            yo[low * OVER : (low + count) * OVER, :] = exact_dot(
                gather[0 : count * OVER, :], stack
            ).astype(jnp.bfloat16)
        part = pl.ds(half * half_width, half_width)
        for slot in CARRIED:
            if low <= slot < low + count:
                number = CARRIED.index(slot)
                other = twin(slot)
                send(
                    ym.at[main(other), part],
                    sib_m.at[number, :, part],
                    siby_send.at[number, half],
                    siby_recv.at[number, half],
                    sibling,
                )
                if half:
                    send(
                        yo.at[over(other), :],
                        sib_o.at[number],
                        siby_send.at[number, 2],
                        siby_recv.at[number, 2],
                        sibling,
                    )

    pump(2 * PIECES - progress[0])
    for index in (0, 1, 4, 5):
        arrived(moved[index][1], w_recv.at[index])
    for line in range(4):
        for n in range(pieces):
            chunk = line * pieces + n
            tall[line * 16 + n : line * 16 + n + 1, :] = wide[0:1, chunk * HD : (chunk + 1) * HD]
        tall[line * 16 + pieces : (line + 1) * 16, :] = jnp.zeros((16 - pieces, HD), jnp.float32)
    for step in (0, 1, 2, 3):
        fetch_shared(step)
        hidden_part(step)
        pump(1)
    landed(major(4), aga_recv, 3)
    share(major(4))
    fetch_shared(4)
    hidden_part(4)
    pump(2 * PIECES + PIECES // 2 - progress[0])
    arrived(down_half[0], w_recv.at[2])

    def summed(own, others):
        value = own.astype(jnp.float32)
        for other in others:
            value = value + other.astype(jnp.float32)
        return value

    def await_parts(slot, extras, half):
        number = CARRIED.index(slot)
        part = pl.ds(half * half_width, half_width)
        arrived(sib_m.at[number, :, part], siby_recv.at[number, half])
        for ref_m, ref_o, spot, sems in extras:
            arrived(ref_m.at[spot, :, part], sems.at[spot, half])
        if half:
            arrived(sib_o.at[number], siby_recv.at[number, 2])
            for ref_m, ref_o, spot, sems in extras:
                arrived(ref_o.at[spot], sems.at[spot, 2])

    def block(slot, extras, lanes):
        number = CARRIED.index(slot)
        return summed(
            ym[main(slot), lanes],
            [sib_m[number, :, lanes]] + [extra[0][extra[2], :, lanes] for extra in extras],
        )

    def tiles(slot, extras):
        number = CARRIED.index(slot)
        return summed(yo[over(slot), :], [sib_o[number]] + [extra[1][extra[2]] for extra in extras])

    def hop(slot, extras, half, goal_m, goal_o, send_sem, recv_sem, number, device):
        await_parts(slot, extras, half)

        @pl.loop(0, half_width // 768)
        def _(n):
            lanes = lanes_of(half, n)
            ym[main(slot), lanes] = block(slot, extras, lanes).astype(jnp.bfloat16)

        part = pl.ds(half * half_width, half_width)
        send(
            ym.at[main(slot), part],
            goal_m.at[number, :, part],
            send_sem.at[number, half],
            recv_sem.at[number, half],
            device,
        )
        if half:
            yo[over(slot), :] = tiles(slot, extras).astype(jnp.bfloat16)
            send(
                yo.at[over(slot), :],
                goal_o.at[number],
                send_sem.at[number, 2],
                recv_sem.at[number, 2],
                device,
            )

    def hop_a(k, half):
        extras = [(rxa_m, rxa_o, k, rsa_recv)] if k < 4 else []
        hop(major(k), extras, half, rxa_m, rxa_o, rsa_send, rsa_recv, k - 1, behind)

    def hop_b(k, half):
        extras = [(rxb_m, rxb_o, k, rsb_recv)] if k < 3 else []
        hop(minor(k), extras, half, rxb_m, rxb_o, rsb_send, rsb_recv, k - 1, ahead)

    def give_back(step, half):
        spot = lax.rem(place + lax.div(step, 2), 4)
        part = 2 * half + lax.rem(tensor + step, 2)
        other = spot * 4 + part
        return other, eo_m.at[rows_of(spot), columns_of(part)], ret_m.at[rows_of(rank), :]

    def give_all(half, start):
        @pl.loop(0, 8)
        def _(step):
            other, src, dst = give_back(step, half)

            @pl.when(other != rank)
            def _():
                copy = pltpu.make_async_remote_copy(
                    src_ref=src,
                    dst_ref=dst,
                    send_sem=ret_send.at[half * 8 + step, 0],
                    recv_sem=ret_recv.at[0],
                    device_id=member(other),
                    device_id_type=MESH,
                )
                if start:
                    copy.start()
                else:
                    copy.wait_send()

            if start:

                @pl.when(other == rank)
                def _():
                    pltpu.make_async_copy(src, dst, ret_recv.at[0]).start()

    def give_over(step):
        other = lax.rem(rank + step, GROUP)
        return pltpu.make_async_remote_copy(
            src_ref=eo_o.at[rows_of(other), :],
            dst_ref=ret_o.at[rows_of(rank), :],
            send_sem=ret_send.at[step, 1],
            recv_sem=ret_recv.at[1],
            device_id=member(other),
            device_id_type=MESH,
        )

    def finish(half):
        last = [(rxb_m, rxb_o, 0, rsb_recv), (rxa_m, rxa_o, 0, rsa_recv)]
        await_parts(OWN, last, half)

        @pl.loop(0, half_width // 768)
        def _(n):
            lanes = lanes_of(half, n)
            eo_m[:, lanes] = (block(OWN, last, lanes) * wide[0:1, lanes]).astype(jnp.bfloat16)

        if half:
            value = tiles(OWN, last)
            for n in range(4):
                eo_o[n * 64 : (n + 1) * 64, :] = (
                    value[n * 64 : (n + 1) * 64, :] * tall[...]
                ).astype(jnp.bfloat16)
        give_all(half, True)
        if half:
            pltpu.make_async_copy(
                eo_o.at[rows_of(rank), :], ret_o.at[rows_of(rank), :], ret_recv.at[1]
            ).start()

            @pl.loop(1, GROUP)
            def _(step):
                give_over(step).start()

    down_part(4, 0)
    hop_a(4, 0)
    down_part(3, 0)
    hop_b(3, 0)
    for step in (2, 1, 0):
        pump(1)
        down_part(step, 0)
    hop_a(3, 0)
    hop_b(2, 0)
    pump(1)
    hop_a(2, 0)
    hop_b(1, 0)
    pump(n_pieces)
    arrived(down_half[1], w_recv.at[3])
    down_part(4, 1)
    hop_a(4, 1)
    down_part(3, 1)
    hop_b(3, 1)
    hop_a(1, 0)
    down_part(2, 1)
    hop_a(3, 1)
    hop_b(2, 1)
    down_part(1, 1)
    hop_a(2, 1)
    hop_b(1, 1)
    down_part(0, 1)
    finish(0)
    hop_a(1, 1)
    finish(1)

    expert_id = iotas(rows, EXPERTS)[1]
    hits = [expert_id == upright(routes_ref[k : k + 1, :]) for k in range(2)]
    first, second = iotas(rows, rows)
    both = one_hot(jnp.logical_or(hits[0], hits[1]))
    token_ranks = exact_dot(one_hot(second < first), both)
    row, col = iotas(EXPERTS, EXPERTS * MAIN)
    expand = one_hot((col >> 4) == row)
    slot_rank = (iotas(rows, EXPERTS * MAIN)[1] & 15).astype(jnp.float32)
    selects = []
    for k in range(2):
        own_ranks = jnp.where(hits[k], token_ranks, -1.0)
        wide_ranks = exact_dot(own_ranks.astype(jnp.bfloat16), expand)
        selects.append((one_hot(wide_ranks == slot_rank), one_hot(own_ranks == float(MAIN))))
    row, col = iotas(EXPERTS * pieces, EXPERTS * TILE_ROWS)
    unshuffle = one_hot((((row & 15) << 4) | (row >> 4)) == col)

    arrived(ret_m, ret_recv.at[0])
    arrived(ret_o, ret_recv.at[1])
    back = exact_dot(unshuffle, ret_o[...]).astype(jnp.bfloat16)
    back = jnp.concatenate(
        [back[n * EXPERTS : (n + 1) * EXPERTS, :] for n in range(pieces)], axis=1
    )
    routed = jnp.zeros((rows, quarter), jnp.float32)
    for k in range(2):
        picked = exact_dot(selects[k][0], ret_m[...]) + exact_dot(selects[k][1], back)
        routed = routed + picked * upright(weight_ref[k : k + 1, :])
    out_ref[...] = (hidden[...] + routed).astype(jnp.bfloat16)

    for copy in pending:
        copy.wait_send()
    for step in (1, 2, 3):
        tell(step).wait_send()

    @pl.loop(1, GROUP)
    def _(step):
        for copy in dispatch(step) + [give_over(step)]:
            copy.wait_send()

    for half in range(2):
        give_all(half, False)

    @pl.when(swapping)
    def _():
        for index in (4, 5):
            swap(index).wait_send()
        for number in range(n_pieces - IN_FLIGHT, n_pieces):
            load(number).wait_send()


def layer(
    queries, keys, values, residual, norm_gain, routes, route_weight, w_gate, w_up, w_down, scale_hidden, scale_out
):
    rows, quarter = residual.shape
    _, width, hid_dev = w_gate.shape
    length = rows * N_CTX
    vmem = pl.BlockSpec(memory_space=pltpu.VMEM)
    hbm = pl.BlockSpec(memory_space=pl.ANY)
    half = jnp.bfloat16
    dma = pltpu.SemaphoreType.DMA
    return pl.pallas_call(
        layer_kernel,
        out_shape=jax.ShapeDtypeStruct((rows, quarter), half),
        in_specs=[vmem] * 3 + [hbm] * 9,
        out_specs=vmem,
        scratch_shapes=[
            pltpu.VMEM((rows, quarter), half),
            pltpu.VMEM((rows, quarter), half),
            pltpu.VMEM((length, HD), half),
            pltpu.VMEM((length, HD), half),
            pltpu.VMEM((length, HD), half),
            pltpu.VMEM((length, HD), half),
            pltpu.VMEM((16 * SLOT, width), half),
            pltpu.VMEM((16 * OVER, HD), half),
            pltpu.VMEM((16 * SLOT, width), half),
            pltpu.VMEM((16 * OVER, HD), half),
            pltpu.VMEM((8, SLOT, width), half),
            pltpu.VMEM((8, OVER, HD), half),
            pltpu.VMEM((4, SLOT, width), half),
            pltpu.VMEM((4, OVER, HD), half),
            pltpu.VMEM((3, SLOT, width), half),
            pltpu.VMEM((3, OVER, HD), half),
            pltpu.VMEM((width, 2 * hid_dev), half),
            pltpu.VMEM((hid_dev, width), half),
            pltpu.VMEM((1, width), jnp.float32),
            pltpu.VMEM((2, hid_dev), jnp.float32),
            pltpu.VMEM((64, HD), jnp.float32),
            pltpu.VMEM((5 * 272, hid_dev), half),
            pltpu.VMEM((272, 2 * hid_dev), jnp.float32),
            pltpu.VMEM((rows, quarter), jnp.float32),
            pltpu.VMEM((EXPERTS * MAIN, quarter), half),
            pltpu.VMEM((EXPERTS * TILE_ROWS, HD), half),
            pltpu.VMEM((SLOT, width), half),
            pltpu.VMEM((OVER, HD), half),
            pltpu.VMEM((EXPERTS * MAIN, quarter), half),
            pltpu.VMEM((EXPERTS * TILE_ROWS, HD), half),
            pltpu.VMEM((16, width), half),
            pltpu.VMEM((80, width), half),
            pltpu.VMEM((36 * 16, 4 * OVER), half),
            pltpu.VMEM((4 * OVER, 36 * 16), half),
            pltpu.VMEM((4, 8, rows), jnp.float32),
            dma((6,)),
            dma((6,)),
            dma((4,)),
            dma((4,)),
            dma((2,)),
            dma((GROUP, 2)),
            dma((4, 2)),
            dma((4, 2)),
            dma((3, 2)),
            dma((3, 2)),
            dma((8, 2)),
            dma((8, 2)),
            dma((8, 3)),
            dma((8, 3)),
            dma((4, 3)),
            dma((4, 3)),
            dma((3, 3)),
            dma((3, 3)),
            dma((2,)),
            dma((GROUP, 2)),
            dma((3 * PIECES,)),
            dma((3,)),
            dma((HEADS_HERE, 3)),
            dma((N_CTX,)),
            dma,
            dma,
        ],
        compiler_params=pltpu.CompilerParams(
            collective_id=0, has_side_effects=True, vmem_limit_bytes=60 * 1024 * 1024
        ),
        cost_estimate=pl.CostEstimate(
            flops=6 * 1088 * width * hid_dev + 2 * length * length * HD, bytes_accessed=12 * 10**6, transcendentals=10**6
        ),
    )(
        norm_gain.reshape(1, quarter),
        routes.T,
        route_weight.T,
        residual,
        queries,
        keys,
        values,
        w_gate,
        w_up,
        w_down,
        scale_hidden,
        scale_out,
    )


def solution(mesh):
    in_specs = (
        P(("dp", "context"), "tensor"),
        P(("dp", "context"), "tensor"),
        P(("dp", "context"), "tensor"),
        P(("dp", "context"), "tensor"),
        P("tensor"),
        P(("dp", "context"), None),
        P(("dp", "context"), None),
        P(("dp", "tensor"), None, "context"),
        P(("dp", "tensor"), None, "context"),
        P(("dp", "tensor"), "context", None),
        P(("dp", "tensor"), None, "context"),
        P(("dp", "tensor"), None),
    )
    out_specs = P(("dp", "context"), "tensor")
    return jax.shard_map(layer, mesh=mesh, in_specs=in_specs, out_specs=out_specs, check_vma=False)
```

```python
import math

import jax
import jax.numpy as jnp
from jax import lax
from jax.experimental import pallas as pl
from jax.experimental.pallas import tpu as pltpu
from jax.sharding import PartitionSpec as P

D = 4608
HD = 128
EXPERTS = 16
EPS = 1e-06
NEG = -1e30
PIECES = 12
IN_FLIGHT = 5
EARLY = 8
N_CTX = 16
HEADS_HERE = 9
MESH = pl.DeviceIdType.MESH
EXP_SCALE = math.log2(math.e) / math.sqrt(HD)


def head_owner(head, core):
    return lax.rem(lax.div(head * N_CTX, HEADS_HERE) + 8 * core, N_CTX)


def attention_phase(
    q_ref, k_ref, v_ref, out_ref, qs, ks, vs, ob, recv_sem, send_sem, out_send, out_recv, pump, prepare
):
    ctx = lax.axis_index("context")
    core = lax.rem(lax.axis_index("dp"), 2)
    rows = q_ref.shape[0]
    my_rows = pl.ds(pl.multiple_of(ctx * rows, rows), rows)
    sources = (k_ref, q_ref, v_ref)
    targets = (ks, qs, vs)

    def scatter(step, start):
        head = lax.rem(ctx + step, HEADS_HERE)
        owner = head_owner(head, core)
        columns = pl.ds(pl.multiple_of(head * HD, HD), HD)
        for index in range(3):
            src = sources[index].at[:, columns]
            dst = targets[index].at[my_rows, :]

            @pl.when(owner != ctx)
            def _():
                copy = pltpu.make_async_remote_copy(
                    src_ref=src,
                    dst_ref=dst,
                    send_sem=send_sem.at[step, index],
                    recv_sem=recv_sem.at[index],
                    device_id={"context": owner},
                    device_id_type=MESH,
                )
                if start:
                    copy.start()
                else:
                    copy.wait_send()

            if start:

                @pl.when(owner == ctx)
                def _():
                    pltpu.make_async_copy(src, dst, recv_sem.at[index]).start()

    @pl.loop(0, HEADS_HERE)
    def _(step):
        scatter(step, True)

    pump(0, 4)
    prepare()

    base = lax.rem(ctx + 8 * core, N_CTX)
    my_head = lax.div(base * HEADS_HERE + N_CTX - 1, N_CTX)
    active = jnp.logical_and(
        my_head < HEADS_HERE, lax.div(my_head * N_CTX, HEADS_HERE) == base
    )
    head_columns = pl.ds(pl.multiple_of(lax.rem(my_head, HEADS_HERE) * HD, HD), HD)

    def give(block, start):
        src = ob.at[pl.ds(block * rows, rows), :]
        dst = out_ref.at[:, head_columns]

        @pl.when(ctx != block)
        def _():
            copy = pltpu.make_async_remote_copy(
                src_ref=src,
                dst_ref=dst,
                send_sem=out_send.at[block],
                recv_sem=out_recv,
                device_id={"context": block},
                device_id_type=MESH,
            )
            if start:
                copy.start()
            else:
                copy.wait_send()

        if start:

            @pl.when(ctx == block)
            def _():
                pltpu.make_async_copy(src, dst, out_recv).start()

    @pl.when(active)
    def _():
        for index in range(3):
            pltpu.make_async_copy(targets[index], targets[index], recv_sem.at[index]).wait()
        tile = 2 * rows
        contract = (((1,), (1,)), ((), ()))
        causal = lax.broadcasted_iota(jnp.int32, (tile, tile), 0) >= lax.broadcasted_iota(
            jnp.int32, (tile, tile), 1
        )
        for number in range(N_CTX // 2 - 1, -1, -1):
            low, high = number * tile, (number + 1) * tile
            query = qs[low:high, :]
            own = lax.dot_general(query, ks[low:high, :], contract, preferred_element_type=jnp.float32)
            own = jnp.where(causal, own, NEG)
            top = jnp.max(own, axis=1, keepdims=True)
            if number:
                past = lax.dot_general(
                    query, ks[0:low, :], contract, preferred_element_type=jnp.float32
                )
                top = jnp.maximum(top, jnp.max(past, axis=1, keepdims=True))
            own = jnp.exp2((own - top) * EXP_SCALE)
            total = jnp.sum(own, axis=1, keepdims=True)
            result = jnp.dot(
                own.astype(jnp.bfloat16), vs[low:high, :], preferred_element_type=jnp.float32
            )
            if number:
                past = jnp.exp2((past - top) * EXP_SCALE)
                total = total + jnp.sum(past, axis=1, keepdims=True)
                result = result + jnp.dot(
                    past.astype(jnp.bfloat16), vs[0:low, :], preferred_element_type=jnp.float32
                )
            ob[low:high, :] = (result / total).astype(jnp.bfloat16)
            give(2 * number + 1, True)
            give(2 * number, True)
            if number in (6, 4):
                pump(4 + (6 - number) // 2, 1)
        pump(6, EARLY - 6)

    @pl.when(jnp.logical_not(active))
    def _():
        pump(4, EARLY - 4)

    @pl.loop(0, HEADS_HERE)
    def _(step):
        scatter(step, False)

    @pl.when(active)
    def _():
        for block in range(N_CTX):
            give(block, False)

    pltpu.make_async_copy(out_ref, out_ref, out_recv).wait()


MAIN = 16
TILE_ROWS = 16
SLOT = 64
OVER = 256
GROUP = 16
N_Z = 8
OWN, SIB_OWN = 0, 1


def major(k):
    return 14 if k == 4 else 4 * k - 2


def minor(k):
    return 4 * k - 1


def twin(slot):
    return slot + 1 if slot in (0, 14) else slot + 2


CARRIED = [OWN] + [s for k in (1, 2, 3) for s in (major(k), minor(k))] + [major(4)]
STEPS = [(0, 2), (2, 4), (6, 4), (10, 4), (14, 2)]


def arrived(ref, sem):
    pltpu.make_async_copy(ref, ref, sem).wait()


def one_hot(hit):
    return jnp.where(hit, 1.0, 0.0).astype(jnp.bfloat16)


def exact_dot(left, right):
    return jnp.dot(left, right, preferred_element_type=jnp.float32)


def iotas(rows, columns):
    return (
        lax.broadcasted_iota(jnp.int32, (rows, columns), 0),
        lax.broadcasted_iota(jnp.int32, (rows, columns), 1),
    )


def layer_kernel(
    gain_ref,
    routes_ref,
    weight_ref,
    residual_ref,
    q_ref,
    k_ref,
    v_ref,
    gate_all,
    up_all,
    down_all,
    inner_all,
    wide_own,
    out_ref,
    residual,
    attended,
    qs,
    ks,
    vs,
    ob,
    xm,
    xo,
    ym,
    yo,
    sib_m,
    sib_o,
    rxa_m,
    rxa_o,
    rxb_m,
    rxb_o,
    w1,
    wd,
    wide,
    inner,
    tall,
    act,
    gates,
    hidden,
    disp_m,
    disp_o,
    eo_m,
    eo_o,
    ret_m,
    ret_o,
    over_x,
    over_y,
    pick_m,
    pick_o,
    spread,
    gather,
    squares,
    w_recv,
    w_send,
    sq_recv,
    sq_send,
    disp_recv,
    disp_send,
    aga_recv,
    aga_send,
    agb_recv,
    agb_send,
    sibx_recv,
    sibx_send,
    siby_recv,
    siby_send,
    rsa_recv,
    rsa_send,
    rsb_recv,
    rsb_send,
    ret_recv,
    ret_send,
    piece_send,
    attn_recv,
    attn_send,
    out_send,
    out_recv,
    res_recv,
):
    dp, ctx, tensor = lax.axis_index("dp"), lax.axis_index("context"), lax.axis_index("tensor")
    core, y_hi = lax.rem(dp, 2), lax.div(dp, 2)
    z, y_lo = lax.rem(ctx, N_Z), lax.div(ctx, N_Z)
    sign = 1 - 2 * core
    place = y_hi * 2 + y_lo
    rank = place * 4 + tensor
    rows, quarter = residual_ref.shape
    width = xm.shape[1]
    hid_dev = wd.shape[0]
    gate_own, up_own, down_own, inner_own = (
        ref.at[0] for ref in (gate_all, up_all, down_all, inner_all)
    )

    def member(number):
        other = lax.div(number, 4)
        return {
            "dp": lax.div(other, 2) * 2 + core,
            "context": lax.rem(other, 2) * N_Z + z,
            "tensor": lax.rem(number, 4),
        }

    ahead = {"context": y_lo * N_Z + lax.rem(z + sign + N_Z, N_Z)}
    behind = {"context": y_lo * N_Z + lax.rem(z - sign + N_Z, N_Z)}
    sibling = {"dp": y_hi * 2 + 1 - core}
    diagonal = {"dp": y_hi * 2 + 1 - core, "context": (1 - y_lo) * N_Z + z}

    barrier = pltpu.get_barrier_semaphore()
    for other in (ahead, behind, sibling, diagonal):
        pl.semaphore_signal(barrier, inc=1, device_id=other, device_id_type=MESH)

    @pl.loop(1, GROUP)
    def _(step):
        pl.semaphore_signal(
            barrier, inc=1, device_id=member(lax.rem(rank + step, GROUP)), device_id_type=MESH
        )

    @pl.loop(1, N_CTX)
    def _(step):
        pl.semaphore_signal(
            barrier, inc=1, device_id={"context": lax.rem(ctx + step, N_CTX)}, device_id_type=MESH
        )

    load_residual = pltpu.make_async_copy(residual_ref, residual, res_recv)
    load_residual.start()
    pl.semaphore_wait(barrier, GROUP + N_CTX + 2)

    pending = []

    def send(src, dst, send_sem, recv_sem, device):
        copy = pltpu.make_async_remote_copy(
            src_ref=src,
            dst_ref=dst,
            send_sem=send_sem,
            recv_sem=recv_sem,
            device_id=device,
            device_id_type=MESH,
        )
        copy.start()
        pending.append(copy)

    swapping = core != y_lo
    gate_part = w1.at[:, pl.ds(0, hid_dev)]
    up_part = w1.at[:, pl.ds(hid_dev, hid_dev)]
    half_width = width // 2
    down_half = [wd.at[:, pl.ds(half * half_width, half_width)] for half in range(2)]
    moved = (
        (gate_own, gate_part),
        (up_own, up_part),
        (down_own.at[:, pl.ds(0, half_width)], down_half[0]),
        (down_own.at[:, pl.ds(half_width, half_width)], down_half[1]),
        (inner_own, inner),
        (wide_own, wide),
    )

    def swap(index):
        return pltpu.make_async_remote_copy(
            src_ref=moved[index][0],
            dst_ref=moved[index][1],
            send_sem=w_send.at[index],
            recv_sem=w_recv.at[index],
            device_id=diagonal,
            device_id_type=MESH,
        )

    n_pieces = 3 * PIECES
    depth = width // PIECES

    def load(number):
        which, part = number // PIECES, pl.ds(number % PIECES * depth, depth)
        if which < 2:
            src = (gate_own, up_own)[which].at[part, :]
            dst = w1.at[part, pl.ds(which * hid_dev, hid_dev)]
        else:
            src, dst = down_own.at[:, part], wd.at[:, part]
            which += number % PIECES // (PIECES // 2)
        return pltpu.make_async_remote_copy(
            src_ref=src,
            dst_ref=dst,
            send_sem=piece_send.at[number],
            recv_sem=w_recv.at[which],
            device_id=diagonal,
            device_id_type=MESH,
        )

    def pump_at(first, count):
        @pl.when(swapping)
        def _():
            for number in range(first, first + count):
                if number >= IN_FLIGHT:
                    load(number - IN_FLIGHT).wait_send()
                load(number).start()

    progress = [EARLY]

    def pump(count):
        first = progress[0]
        progress[0] = min(first + max(count, 0), n_pieces)
        if progress[0] > first:
            pump_at(first, progress[0] - first)

    @pl.when(swapping)
    def _():
        for index in (4, 5):
            swap(index).start()

    @pl.when(jnp.logical_not(swapping))
    def _():
        for index in range(6):
            pltpu.make_async_copy(moved[index][0], moved[index][1], w_recv.at[index]).start()

    def prepare():
        row, col = iotas(EXPERTS, rows)
        named = jnp.logical_or(row == routes_ref[0:1, :], row == routes_ref[1:2, :])
        first, second = iotas(rows, rows)
        ranks = exact_dot(one_hot(named), one_hot(first < second))
        ranks = jnp.where(named, ranks, -1.0)
        row, col = iotas(EXPERTS * MAIN, EXPERTS)
        widened = exact_dot(one_hot((row >> 4) == col), ranks.astype(jnp.bfloat16))
        row, col = iotas(EXPERTS * MAIN, rows)
        pick_m[...] = one_hot(widened == (row & 15).astype(jnp.float32))
        pick_o[...] = one_hot(ranks == float(MAIN))

    attention_phase(
        q_ref, k_ref, v_ref, attended, qs, ks, vs, ob, attn_recv, attn_send, out_send, out_recv, pump_at, prepare
    )
    load_residual.wait()

    def upright(line):
        return jnp.broadcast_to(line, (rows, rows)).T[:, 0:1]

    state = residual[...].astype(jnp.float32) + attended[...].astype(jnp.float32)
    hidden[...] = state
    own_squares = jnp.sum(state * state, axis=1, keepdims=True)
    squares[tensor] = jnp.broadcast_to(own_squares, (rows, rows)).T[0:8, :]

    def tell(step):
        peer = lax.rem(tensor + step, 4)
        return pltpu.make_async_remote_copy(
            src_ref=squares.at[tensor],
            dst_ref=squares.at[tensor],
            send_sem=sq_send.at[peer],
            recv_sem=sq_recv.at[tensor],
            device_id={"tensor": peer},
            device_id_type=MESH,
        )

    for step in (1, 2, 3):
        tell(step).start()

    pump(1)
    for step in (1, 2, 3):
        peer = lax.rem(tensor + step, 4)
        arrived(squares.at[peer], sq_recv.at[peer])
    total = squares[0] + squares[1] + squares[2] + squares[3]
    inverse = lax.rsqrt(total / D + EPS)
    normed = (hidden[...] * upright(inverse[0:1, :]) * gain_ref[...]).astype(jnp.bfloat16)
    disp_m[...] = exact_dot(pick_m[...], normed).astype(jnp.bfloat16)
    overflow = exact_dot(pick_o[...], normed).astype(jnp.bfloat16)
    pieces = quarter // HD
    stacked = jnp.concatenate(
        [overflow[:, n * HD : (n + 1) * HD] for n in range(pieces)], axis=0
    )
    row, col = iotas(EXPERTS * TILE_ROWS, EXPERTS * pieces)
    shuffle = one_hot((((col & 15) << 4) | (col >> 4)) == row)
    disp_o[...] = exact_dot(shuffle, stacked).astype(jnp.bfloat16)

    def rows_of(number):
        return pl.ds(pl.multiple_of(number * TILE_ROWS, TILE_ROWS), TILE_ROWS)

    def columns_of(number):
        return pl.ds(pl.multiple_of(number * quarter, quarter), quarter)

    def dispatch(step):
        other = lax.rem(rank + step, GROUP)
        pairs = (
            (disp_m.at[rows_of(other), :], xm.at[rows_of(place), columns_of(tensor)]),
            (disp_o.at[rows_of(other), :], xo.at[rows_of(rank), :]),
        )
        return [
            pltpu.make_async_remote_copy(
                src_ref=src,
                dst_ref=dst,
                send_sem=disp_send.at[step, index],
                recv_sem=disp_recv.at[index],
                device_id=member(other),
                device_id_type=MESH,
            )
            for index, (src, dst) in enumerate(pairs)
        ]

    pltpu.make_async_copy(
        disp_m.at[rows_of(rank), :], xm.at[rows_of(place), columns_of(tensor)], disp_recv.at[0]
    ).start()
    pltpu.make_async_copy(
        disp_o.at[rows_of(rank), :], xo.at[rows_of(rank), :], disp_recv.at[1]
    ).start()

    @pl.loop(1, GROUP)
    def _(step):
        for copy in dispatch(step):
            copy.start()

    row, col = iotas(36 * 16, 4 * OVER)
    chunk, inside = col >> 8, col & 255
    source, part, piece = inside >> 6, (inside >> 4) & 3, inside & 15
    goal = (part * pieces + piece) * 16 + chunk * 4 + source
    spread[...] = one_hot(jnp.logical_and(piece < pieces, goal == row))
    row, col = iotas(4 * OVER, 36 * 16)
    chunk, inside = row >> 8, row & 255
    source, part, piece = inside >> 6, (inside >> 4) & 3, inside & 15
    goal = (part * pieces + piece) * 16 + chunk * 4 + source
    gather[...] = one_hot(jnp.logical_and(piece < pieces, goal == col))

    def main(slot):
        return pl.ds(slot * SLOT, SLOT)

    def over(slot):
        return pl.ds(slot * OVER, OVER)

    def pass_on(slot, goal, send_sem, recv_sem, number, device):
        send(xm.at[main(slot), :], xm.at[main(goal), :], send_sem.at[number, 0], recv_sem.at[number, 0], device)
        send(xo.at[over(slot), :], xo.at[over(goal), :], send_sem.at[number, 1], recv_sem.at[number, 1], device)

    def landed(slot, recv_sem, number):
        arrived(xm.at[main(slot), :], recv_sem.at[number, 0])
        arrived(xo.at[over(slot), :], recv_sem.at[number, 1])

    def share(slot):
        pass_on(slot, twin(slot), sibx_send, sibx_recv, CARRIED.index(slot), sibling)

    pump(3)
    arrived(xm.at[main(OWN), :], disp_recv.at[0])
    arrived(xo.at[over(OWN), :], disp_recv.at[1])
    pass_on(OWN, major(1), aga_send, aga_recv, 0, ahead)
    pass_on(OWN, minor(1), agb_send, agb_recv, 0, behind)
    share(OWN)
    def fetch_shared(step):
        low, count = STEPS[step]
        for slot in CARRIED:
            if low <= slot < low + count:
                landed(twin(slot), sibx_recv, CARRIED.index(slot))

    def step_rows(step):
        return STEPS[step][1] * SLOT

    def rows_in(step):
        low = STEPS[step][0] * SLOT
        return jnp.concatenate(
            [xm[low : low + step_rows(step), :], over_x[step * 16 : step * 16 + 16, :]], axis=0
        )

    def gate_products(step):
        low, count = STEPS[step]
        size = step_rows(step) + 16
        tiles = xo[low * OVER : (low + count) * OVER, :]
        stack = exact_dot(spread[:, 0 : count * OVER], tiles).astype(jnp.bfloat16)
        for n in range(36):
            over_x[step * 16 : step * 16 + 16, n * HD : (n + 1) * HD] = stack[n * 16 : (n + 1) * 16, :]
        gates[step * 272 : step * 272 + size, :] = exact_dot(rows_in(step), w1[:, 0:hid_dev])

    def up_products(step):
        size = step_rows(step) + 16
        up = exact_dot(rows_in(step), w1[:, hid_dev : 2 * hid_dev]) * inner[1:2, :]
        gate = gates[step * 272 : step * 272 + size, :] * inner[0:1, :]
        act[step * 272 : step * 272 + size, :] = (gate / (1.0 + jnp.exp(-gate)) * up).astype(
            jnp.bfloat16
        )

    def lanes_of(half, n):
        start = half * half_width + n * 768
        return pl.ds(start if isinstance(n, int) else pl.multiple_of(start, 256), 768)

    def down_part(step, half):
        low, count = STEPS[step]
        size = step_rows(step)

        @pl.loop(0, half_width // 768)
        def _(n):
            lanes = lanes_of(half, n)
            result = exact_dot(act[step * 272 : step * 272 + size + 16, :], wd[:, lanes])
            result = result.astype(jnp.bfloat16)
            ym[low * SLOT : low * SLOT + size, lanes] = result[0:size, :]
            over_y[step * 16 : step * 16 + 16, lanes] = result[size:, :]

        if half:
            stack = jnp.concatenate(
                [over_y[step * 16 : step * 16 + 16, n * HD : (n + 1) * HD] for n in range(36)], axis=0
            )
            yo[low * OVER : (low + count) * OVER, :] = exact_dot(
                gather[0 : count * OVER, :], stack
            ).astype(jnp.bfloat16)
        part = pl.ds(half * half_width, half_width)
        for slot in CARRIED:
            if low <= slot < low + count:
                number = CARRIED.index(slot)
                other = twin(slot)
                send(
                    ym.at[main(other), part],
                    sib_m.at[number, :, part],
                    siby_send.at[number, half],
                    siby_recv.at[number, half],
                    sibling,
                )
                if half:
                    send(
                        yo.at[over(other), :],
                        sib_o.at[number],
                        siby_send.at[number, 2],
                        siby_recv.at[number, 2],
                        sibling,
                    )

    for k in (1, 2, 3):
        pump(6)
        landed(major(k), aga_recv, k - 1)
        pass_on(major(k), major(k + 1), aga_send, aga_recv, k, ahead)
        share(major(k))
        landed(minor(k), agb_recv, k - 1)
        if k < 3:
            pass_on(minor(k), minor(k + 1), agb_send, agb_recv, k, behind)
        share(minor(k))
        if k == 1:
            arrived(gate_part, w_recv.at[0])
        fetch_shared(k - 1)
        gate_products(k - 1)
    fetch_shared(3)
    gate_products(3)
    pump(2 * PIECES - progress[0])
    for index in (1, 4, 5):
        arrived(moved[index][1], w_recv.at[index])
    for line in range(4):
        for n in range(pieces):
            chunk = line * pieces + n
            tall[line * 16 + n : line * 16 + n + 1, :] = wide[0:1, chunk * HD : (chunk + 1) * HD]
        tall[line * 16 + pieces : (line + 1) * 16, :] = jnp.zeros((16 - pieces, HD), jnp.float32)
    for step in (0, 1, 2):
        up_products(step)
        pump(1)
    landed(major(4), aga_recv, 3)
    share(major(4))
    up_products(3)
    pump(1)
    fetch_shared(4)
    gate_products(4)
    up_products(4)
    pump(2 * PIECES + PIECES // 2 - progress[0])
    arrived(down_half[0], w_recv.at[2])

    def summed(own, others):
        value = own.astype(jnp.float32)
        for other in others:
            value = value + other.astype(jnp.float32)
        return value

    def await_parts(slot, extras, half):
        number = CARRIED.index(slot)
        part = pl.ds(half * half_width, half_width)
        arrived(sib_m.at[number, :, part], siby_recv.at[number, half])
        for ref_m, ref_o, spot, sems in extras:
            arrived(ref_m.at[spot, :, part], sems.at[spot, half])
        if half:
            arrived(sib_o.at[number], siby_recv.at[number, 2])
            for ref_m, ref_o, spot, sems in extras:
                arrived(ref_o.at[spot], sems.at[spot, 2])

    def block(slot, extras, lanes):
        number = CARRIED.index(slot)
        return summed(
            ym[main(slot), lanes],
            [sib_m[number, :, lanes]] + [extra[0][extra[2], :, lanes] for extra in extras],
        )

    def tiles(slot, extras):
        number = CARRIED.index(slot)
        return summed(yo[over(slot), :], [sib_o[number]] + [extra[1][extra[2]] for extra in extras])

    def hop(slot, extras, half, goal_m, goal_o, send_sem, recv_sem, number, device):
        await_parts(slot, extras, half)

        @pl.loop(0, half_width // 768)
        def _(n):
            lanes = lanes_of(half, n)
            ym[main(slot), lanes] = block(slot, extras, lanes).astype(jnp.bfloat16)

        part = pl.ds(half * half_width, half_width)
        send(
            ym.at[main(slot), part],
            goal_m.at[number, :, part],
            send_sem.at[number, half],
            recv_sem.at[number, half],
            device,
        )
        if half:
            yo[over(slot), :] = tiles(slot, extras).astype(jnp.bfloat16)
            send(
                yo.at[over(slot), :],
                goal_o.at[number],
                send_sem.at[number, 2],
                recv_sem.at[number, 2],
                device,
            )

    def hop_a(k, half):
        extras = [(rxa_m, rxa_o, k, rsa_recv)] if k < 4 else []
        hop(major(k), extras, half, rxa_m, rxa_o, rsa_send, rsa_recv, k - 1, behind)

    def hop_b(k, half):
        extras = [(rxb_m, rxb_o, k, rsb_recv)] if k < 3 else []
        hop(minor(k), extras, half, rxb_m, rxb_o, rsb_send, rsb_recv, k - 1, ahead)

    def give_back(step, half):
        spot = lax.rem(place + lax.div(step, 2), 4)
        part = 2 * half + lax.rem(tensor + step, 2)
        other = spot * 4 + part
        return other, eo_m.at[rows_of(spot), columns_of(part)], ret_m.at[rows_of(rank), :]

    def give_all(half, start):
        @pl.loop(0, 8)
        def _(step):
            other, src, dst = give_back(step, half)

            @pl.when(other != rank)
            def _():
                copy = pltpu.make_async_remote_copy(
                    src_ref=src,
                    dst_ref=dst,
                    send_sem=ret_send.at[half * 8 + step, 0],
                    recv_sem=ret_recv.at[0],
                    device_id=member(other),
                    device_id_type=MESH,
                )
                if start:
                    copy.start()
                else:
                    copy.wait_send()

            if start:

                @pl.when(other == rank)
                def _():
                    pltpu.make_async_copy(src, dst, ret_recv.at[0]).start()

    def give_over(step):
        other = lax.rem(rank + step, GROUP)
        return pltpu.make_async_remote_copy(
            src_ref=eo_o.at[rows_of(other), :],
            dst_ref=ret_o.at[rows_of(rank), :],
            send_sem=ret_send.at[step, 1],
            recv_sem=ret_recv.at[1],
            device_id=member(other),
            device_id_type=MESH,
        )

    def finish(half):
        last = [(rxb_m, rxb_o, 0, rsb_recv), (rxa_m, rxa_o, 0, rsa_recv)]
        await_parts(OWN, last, half)

        @pl.loop(0, half_width // 768)
        def _(n):
            lanes = lanes_of(half, n)
            eo_m[:, lanes] = (block(OWN, last, lanes) * wide[0:1, lanes]).astype(jnp.bfloat16)

        if half:
            value = tiles(OWN, last)
            for n in range(4):
                eo_o[n * 64 : (n + 1) * 64, :] = (
                    value[n * 64 : (n + 1) * 64, :] * tall[...]
                ).astype(jnp.bfloat16)
        give_all(half, True)
        if half:
            pltpu.make_async_copy(
                eo_o.at[rows_of(rank), :], ret_o.at[rows_of(rank), :], ret_recv.at[1]
            ).start()

            @pl.loop(1, GROUP)
            def _(step):
                give_over(step).start()

    down_part(4, 0)
    hop_a(4, 0)
    down_part(3, 0)
    hop_b(3, 0)
    for step in (2, 1, 0):
        pump(1)
        down_part(step, 0)
    hop_a(3, 0)
    hop_b(2, 0)
    pump(1)
    hop_a(2, 0)
    hop_b(1, 0)
    pump(n_pieces)
    arrived(down_half[1], w_recv.at[3])
    down_part(4, 1)
    hop_a(4, 1)
    down_part(3, 1)
    hop_b(3, 1)
    hop_a(1, 0)
    down_part(2, 1)
    hop_a(3, 1)
    hop_b(2, 1)
    down_part(1, 1)
    hop_a(2, 1)
    hop_b(1, 1)
    down_part(0, 1)
    finish(0)
    hop_a(1, 1)
    finish(1)

    expert_id = iotas(rows, EXPERTS)[1]
    hits = [expert_id == upright(routes_ref[k : k + 1, :]) for k in range(2)]
    first, second = iotas(rows, rows)
    both = one_hot(jnp.logical_or(hits[0], hits[1]))
    token_ranks = exact_dot(one_hot(second < first), both)
    row, col = iotas(EXPERTS, EXPERTS * MAIN)
    expand = one_hot((col >> 4) == row)
    slot_rank = (iotas(rows, EXPERTS * MAIN)[1] & 15).astype(jnp.float32)
    selects = []
    for k in range(2):
        own_ranks = jnp.where(hits[k], token_ranks, -1.0)
        wide_ranks = exact_dot(own_ranks.astype(jnp.bfloat16), expand)
        selects.append((one_hot(wide_ranks == slot_rank), one_hot(own_ranks == float(MAIN))))
    row, col = iotas(EXPERTS * pieces, EXPERTS * TILE_ROWS)
    unshuffle = one_hot((((row & 15) << 4) | (row >> 4)) == col)

    arrived(ret_m, ret_recv.at[0])
    arrived(ret_o, ret_recv.at[1])
    back = exact_dot(unshuffle, ret_o[...]).astype(jnp.bfloat16)
    back = jnp.concatenate(
        [back[n * EXPERTS : (n + 1) * EXPERTS, :] for n in range(pieces)], axis=1
    )
    routed = jnp.zeros((rows, quarter), jnp.float32)
    for k in range(2):
        picked = exact_dot(selects[k][0], ret_m[...]) + exact_dot(selects[k][1], back)
        routed = routed + picked * upright(weight_ref[k : k + 1, :])
    out_ref[...] = (hidden[...] + routed).astype(jnp.bfloat16)

    for copy in pending:
        copy.wait_send()
    for step in (1, 2, 3):
        tell(step).wait_send()

    @pl.loop(1, GROUP)
    def _(step):
        for copy in dispatch(step) + [give_over(step)]:
            copy.wait_send()

    for half in range(2):
        give_all(half, False)

    @pl.when(swapping)
    def _():
        for index in (4, 5):
            swap(index).wait_send()
        for number in range(n_pieces - IN_FLIGHT, n_pieces):
            load(number).wait_send()


def layer(
    queries, keys, values, residual, norm_gain, routes, route_weight, w_gate, w_up, w_down, scale_hidden, scale_out
):
    rows, quarter = residual.shape
    _, width, hid_dev = w_gate.shape
    length = rows * N_CTX
    vmem = pl.BlockSpec(memory_space=pltpu.VMEM)
    hbm = pl.BlockSpec(memory_space=pl.ANY)
    half = jnp.bfloat16
    dma = pltpu.SemaphoreType.DMA
    return pl.pallas_call(
        layer_kernel,
        out_shape=jax.ShapeDtypeStruct((rows, quarter), half),
        in_specs=[vmem] * 3 + [hbm] * 9,
        out_specs=vmem,
        scratch_shapes=[
            pltpu.VMEM((rows, quarter), half),
            pltpu.VMEM((rows, quarter), half),
            pltpu.VMEM((length, HD), half),
            pltpu.VMEM((length, HD), half),
            pltpu.VMEM((length, HD), half),
            pltpu.VMEM((length, HD), half),
            pltpu.VMEM((16 * SLOT, width), half),
            pltpu.VMEM((16 * OVER, HD), half),
            pltpu.VMEM((16 * SLOT, width), half),
            pltpu.VMEM((16 * OVER, HD), half),
            pltpu.VMEM((8, SLOT, width), half),
            pltpu.VMEM((8, OVER, HD), half),
            pltpu.VMEM((4, SLOT, width), half),
            pltpu.VMEM((4, OVER, HD), half),
            pltpu.VMEM((3, SLOT, width), half),
            pltpu.VMEM((3, OVER, HD), half),
            pltpu.VMEM((width, 2 * hid_dev), half),
            pltpu.VMEM((hid_dev, width), half),
            pltpu.VMEM((1, width), jnp.float32),
            pltpu.VMEM((2, hid_dev), jnp.float32),
            pltpu.VMEM((64, HD), jnp.float32),
            pltpu.VMEM((5 * 272, hid_dev), half),
            pltpu.VMEM((5 * 272, hid_dev), jnp.float32),
            pltpu.VMEM((rows, quarter), jnp.float32),
            pltpu.VMEM((EXPERTS * MAIN, quarter), half),
            pltpu.VMEM((EXPERTS * TILE_ROWS, HD), half),
            pltpu.VMEM((SLOT, width), half),
            pltpu.VMEM((OVER, HD), half),
            pltpu.VMEM((EXPERTS * MAIN, quarter), half),
            pltpu.VMEM((EXPERTS * TILE_ROWS, HD), half),
            pltpu.VMEM((80, width), half),
            pltpu.VMEM((80, width), half),
            pltpu.VMEM((EXPERTS * MAIN, rows), half),
            pltpu.VMEM((EXPERTS, rows), half),
            pltpu.VMEM((36 * 16, 4 * OVER), half),
            pltpu.VMEM((4 * OVER, 36 * 16), half),
            pltpu.VMEM((4, 8, rows), jnp.float32),
            dma((6,)),
            dma((6,)),
            dma((4,)),
            dma((4,)),
            dma((2,)),
            dma((GROUP, 2)),
            dma((4, 2)),
            dma((4, 2)),
            dma((3, 2)),
            dma((3, 2)),
            dma((8, 2)),
            dma((8, 2)),
            dma((8, 3)),
            dma((8, 3)),
            dma((4, 3)),
            dma((4, 3)),
            dma((3, 3)),
            dma((3, 3)),
            dma((2,)),
            dma((GROUP, 2)),
            dma((3 * PIECES,)),
            dma((3,)),
            dma((HEADS_HERE, 3)),
            dma((N_CTX,)),
            dma,
            dma,
        ],
        compiler_params=pltpu.CompilerParams(
            collective_id=0, has_side_effects=True, vmem_limit_bytes=60 * 1024 * 1024
        ),
        cost_estimate=pl.CostEstimate(
            flops=6 * 1088 * width * hid_dev + 2 * length * length * HD, bytes_accessed=12 * 10**6, transcendentals=10**6
        ),
    )(
        norm_gain.reshape(1, quarter),
        routes.T,
        route_weight.T,
        residual,
        queries,
        keys,
        values,
        w_gate,
        w_up,
        w_down,
        scale_hidden,
        scale_out,
    )


def solution(mesh):
    in_specs = (
        P(("dp", "context"), "tensor"),
        P(("dp", "context"), "tensor"),
        P(("dp", "context"), "tensor"),
        P(("dp", "context"), "tensor"),
        P("tensor"),
        P(("dp", "context"), None),
        P(("dp", "context"), None),
        P(("dp", "tensor"), None, "context"),
        P(("dp", "tensor"), None, "context"),
        P(("dp", "tensor"), "context", None),
        P(("dp", "tensor"), None, "context"),
        P(("dp", "tensor"), None),
    )
    out_specs = P(("dp", "context"), "tensor")
    return jax.shard_map(layer, mesh=mesh, in_specs=in_specs, out_specs=out_specs, check_vma=False)
```

```python
import math

import jax
import jax.numpy as jnp
from jax import lax
from jax.experimental import pallas as pl
from jax.experimental.pallas import tpu as pltpu
from jax.sharding import PartitionSpec as P

D = 4608
HD = 128
EXPERTS = 16
EPS = 1e-06
NEG = -1e30
PIECES = 12
IN_FLIGHT = 5
EARLY = 8
N_CTX = 16
HEADS_HERE = 9
MESH = pl.DeviceIdType.MESH
EXP_SCALE = math.log2(math.e) / math.sqrt(HD)


def head_owner(head, core):
    return lax.rem(lax.div(head * N_CTX, HEADS_HERE) + 8 * core, N_CTX)


def attention_phase(
    q_ref, k_ref, v_ref, out_ref, qs, ks, vs, ob, recv_sem, send_sem, out_send, out_recv, pump, prepare
):
    ctx = lax.axis_index("context")
    core = lax.rem(lax.axis_index("dp"), 2)
    rows = q_ref.shape[0]
    my_rows = pl.ds(pl.multiple_of(ctx * rows, rows), rows)
    sources = (k_ref, q_ref, v_ref)
    targets = (ks, qs, vs)

    def scatter(step, start):
        head = lax.rem(ctx + step, HEADS_HERE)
        owner = head_owner(head, core)
        columns = pl.ds(pl.multiple_of(head * HD, HD), HD)
        for index in range(3):
            src = sources[index].at[:, columns]
            dst = targets[index].at[my_rows, :]

            @pl.when(owner != ctx)
            def _():
                copy = pltpu.make_async_remote_copy(
                    src_ref=src,
                    dst_ref=dst,
                    send_sem=send_sem.at[step, index],
                    recv_sem=recv_sem.at[index],
                    device_id={"context": owner},
                    device_id_type=MESH,
                )
                if start:
                    copy.start()
                else:
                    copy.wait_send()

            if start:

                @pl.when(owner == ctx)
                def _():
                    pltpu.make_async_copy(src, dst, recv_sem.at[index]).start()

    @pl.loop(0, HEADS_HERE)
    def _(step):
        scatter(step, True)

    pump(0, 4)
    prepare()

    base = lax.rem(ctx + 8 * core, N_CTX)
    my_head = lax.div(base * HEADS_HERE + N_CTX - 1, N_CTX)
    active = jnp.logical_and(
        my_head < HEADS_HERE, lax.div(my_head * N_CTX, HEADS_HERE) == base
    )
    head_columns = pl.ds(pl.multiple_of(lax.rem(my_head, HEADS_HERE) * HD, HD), HD)

    def give(block, start):
        src = ob.at[pl.ds(block * rows, rows), :]
        dst = out_ref.at[:, head_columns]

        @pl.when(ctx != block)
        def _():
            copy = pltpu.make_async_remote_copy(
                src_ref=src,
                dst_ref=dst,
                send_sem=out_send.at[block],
                recv_sem=out_recv,
                device_id={"context": block},
                device_id_type=MESH,
            )
            if start:
                copy.start()
            else:
                copy.wait_send()

        if start:

            @pl.when(ctx == block)
            def _():
                pltpu.make_async_copy(src, dst, out_recv).start()

    @pl.when(active)
    def _():
        for index in range(3):
            pltpu.make_async_copy(targets[index], targets[index], recv_sem.at[index]).wait()
        tile = 2 * rows
        contract = (((1,), (1,)), ((), ()))
        causal = lax.broadcasted_iota(jnp.int32, (tile, tile), 0) >= lax.broadcasted_iota(
            jnp.int32, (tile, tile), 1
        )
        for number in range(N_CTX // 2 - 1, -1, -1):
            low, high = number * tile, (number + 1) * tile
            query = qs[low:high, :]
            own = lax.dot_general(query, ks[low:high, :], contract, preferred_element_type=jnp.float32)
            own = jnp.where(causal, own, NEG)
            top = jnp.max(own, axis=1, keepdims=True)
            if number:
                past = lax.dot_general(
                    query, ks[0:low, :], contract, preferred_element_type=jnp.float32
                )
                top = jnp.maximum(top, jnp.max(past, axis=1, keepdims=True))
            own = jnp.exp2((own - top) * EXP_SCALE)
            total = jnp.sum(own, axis=1, keepdims=True)
            result = jnp.dot(
                own.astype(jnp.bfloat16), vs[low:high, :], preferred_element_type=jnp.float32
            )
            if number:
                past = jnp.exp2((past - top) * EXP_SCALE)
                total = total + jnp.sum(past, axis=1, keepdims=True)
                result = result + jnp.dot(
                    past.astype(jnp.bfloat16), vs[0:low, :], preferred_element_type=jnp.float32
                )
            ob[low:high, :] = (result / total).astype(jnp.bfloat16)
            give(2 * number + 1, True)
            give(2 * number, True)
            if number in (6, 4):
                pump(4 + (6 - number) // 2, 1)
        pump(6, EARLY - 6)

    @pl.when(jnp.logical_not(active))
    def _():
        pump(4, EARLY - 4)

    @pl.loop(0, HEADS_HERE)
    def _(step):
        scatter(step, False)

    @pl.when(active)
    def _():
        for block in range(N_CTX):
            give(block, False)

    pltpu.make_async_copy(out_ref, out_ref, out_recv).wait()


MAIN = 16
TILE_ROWS = 16
SLOT = 64
OVER = 256
GROUP = 16
N_Z = 8
OWN, SIB_OWN = 0, 1


def major(k):
    return 14 if k == 4 else 4 * k - 2


def minor(k):
    return 4 * k - 1


def twin(slot):
    return slot + 1 if slot in (0, 14) else slot + 2


CARRIED = [OWN] + [s for k in (1, 2, 3) for s in (major(k), minor(k))] + [major(4)]
STEPS = [(0, 2), (2, 4), (6, 4), (10, 4), (14, 2)]


def arrived(ref, sem):
    pltpu.make_async_copy(ref, ref, sem).wait()


def one_hot(hit):
    return jnp.where(hit, 1.0, 0.0).astype(jnp.bfloat16)


def exact_dot(left, right):
    return jnp.dot(left, right, preferred_element_type=jnp.float32)


def iotas(rows, columns):
    return (
        lax.broadcasted_iota(jnp.int32, (rows, columns), 0),
        lax.broadcasted_iota(jnp.int32, (rows, columns), 1),
    )


def layer_kernel(
    gain_ref,
    routes_ref,
    weight_ref,
    residual_ref,
    q_ref,
    k_ref,
    v_ref,
    gate_all,
    up_all,
    down_all,
    inner_all,
    wide_own,
    out_ref,
    residual,
    attended,
    qs,
    ks,
    vs,
    ob,
    xm,
    xo,
    ym,
    yo,
    sib_m,
    sib_o,
    rxa_m,
    rxa_o,
    rxb_m,
    rxb_o,
    w1,
    wd,
    wide,
    inner,
    tall,
    act,
    gates,
    hidden,
    disp_m,
    disp_o,
    eo_m,
    eo_o,
    ret_m,
    ret_o,
    over_x,
    over_y,
    pick_m,
    pick_o,
    spread,
    gather,
    squares,
    w_recv,
    w_send,
    sq_recv,
    sq_send,
    disp_recv,
    disp_send,
    aga_recv,
    aga_send,
    agb_recv,
    agb_send,
    sibx_recv,
    sibx_send,
    siby_recv,
    siby_send,
    rsa_recv,
    rsa_send,
    rsb_recv,
    rsb_send,
    ret_recv,
    ret_send,
    piece_send,
    attn_recv,
    attn_send,
    out_send,
    out_recv,
    res_recv,
):
    dp, ctx, tensor = lax.axis_index("dp"), lax.axis_index("context"), lax.axis_index("tensor")
    core, y_hi = lax.rem(dp, 2), lax.div(dp, 2)
    z, y_lo = lax.rem(ctx, N_Z), lax.div(ctx, N_Z)
    sign = 1 - 2 * core
    place = y_hi * 2 + y_lo
    rank = place * 4 + tensor
    rows, quarter = residual_ref.shape
    width = xm.shape[1]
    hid_dev = wd.shape[0]
    gate_own, up_own, down_own, inner_own = (
        ref.at[0] for ref in (gate_all, up_all, down_all, inner_all)
    )

    def member(number):
        other = lax.div(number, 4)
        return {
            "dp": lax.div(other, 2) * 2 + core,
            "context": lax.rem(other, 2) * N_Z + z,
            "tensor": lax.rem(number, 4),
        }

    ahead = {"context": y_lo * N_Z + lax.rem(z + sign + N_Z, N_Z)}
    behind = {"context": y_lo * N_Z + lax.rem(z - sign + N_Z, N_Z)}
    sibling = {"dp": y_hi * 2 + 1 - core}
    diagonal = {"dp": y_hi * 2 + 1 - core, "context": (1 - y_lo) * N_Z + z}

    barrier = pltpu.get_barrier_semaphore()
    for other in (ahead, behind, sibling, diagonal):
        pl.semaphore_signal(barrier, inc=1, device_id=other, device_id_type=MESH)

    @pl.loop(1, GROUP)
    def _(step):
        pl.semaphore_signal(
            barrier, inc=1, device_id=member(lax.rem(rank + step, GROUP)), device_id_type=MESH
        )

    @pl.loop(1, N_CTX)
    def _(step):
        pl.semaphore_signal(
            barrier, inc=1, device_id={"context": lax.rem(ctx + step, N_CTX)}, device_id_type=MESH
        )

    load_residual = pltpu.make_async_copy(residual_ref, residual, res_recv)
    load_residual.start()
    pl.semaphore_wait(barrier, GROUP + N_CTX + 2)

    pending = []

    def send(src, dst, send_sem, recv_sem, device):
        copy = pltpu.make_async_remote_copy(
            src_ref=src,
            dst_ref=dst,
            send_sem=send_sem,
            recv_sem=recv_sem,
            device_id=device,
            device_id_type=MESH,
        )
        copy.start()
        pending.append(copy)

    swapping = core != y_lo
    gate_part = w1.at[:, pl.ds(0, hid_dev)]
    up_part = w1.at[:, pl.ds(hid_dev, hid_dev)]
    half_width = width // 2
    down_half = [wd.at[:, pl.ds(half * half_width, half_width)] for half in range(2)]
    moved = (
        (gate_own, gate_part),
        (up_own, up_part),
        (down_own.at[:, pl.ds(0, half_width)], down_half[0]),
        (down_own.at[:, pl.ds(half_width, half_width)], down_half[1]),
        (inner_own, inner),
        (wide_own, wide),
    )

    def swap(index):
        return pltpu.make_async_remote_copy(
            src_ref=moved[index][0],
            dst_ref=moved[index][1],
            send_sem=w_send.at[index],
            recv_sem=w_recv.at[index],
            device_id=diagonal,
            device_id_type=MESH,
        )

    n_pieces = 3 * PIECES
    depth = width // PIECES

    def load(number):
        which, part = number // PIECES, pl.ds(number % PIECES * depth, depth)
        if which < 2:
            src = (gate_own, up_own)[which].at[part, :]
            dst = w1.at[part, pl.ds(which * hid_dev, hid_dev)]
        else:
            src, dst = down_own.at[:, part], wd.at[:, part]
            which += number % PIECES // (PIECES // 2)
        return pltpu.make_async_remote_copy(
            src_ref=src,
            dst_ref=dst,
            send_sem=piece_send.at[number],
            recv_sem=w_recv.at[which],
            device_id=diagonal,
            device_id_type=MESH,
        )

    def pump_at(first, count):
        @pl.when(swapping)
        def _():
            for number in range(first, first + count):
                if number >= IN_FLIGHT:
                    load(number - IN_FLIGHT).wait_send()
                load(number).start()

    progress = [EARLY]

    def pump(count):
        first = progress[0]
        progress[0] = min(first + max(count, 0), n_pieces)
        if progress[0] > first:
            pump_at(first, progress[0] - first)

    @pl.when(swapping)
    def _():
        for index in (4, 5):
            swap(index).start()

    @pl.when(jnp.logical_not(swapping))
    def _():
        for index in range(6):
            pltpu.make_async_copy(moved[index][0], moved[index][1], w_recv.at[index]).start()

    def prepare():
        row, col = iotas(EXPERTS, rows)
        named = jnp.logical_or(row == routes_ref[0:1, :], row == routes_ref[1:2, :])
        first, second = iotas(rows, rows)
        ranks = exact_dot(one_hot(named), one_hot(first < second))
        ranks = jnp.where(named, ranks, -1.0)
        row, col = iotas(EXPERTS * MAIN, EXPERTS)
        widened = exact_dot(one_hot((row >> 4) == col), ranks.astype(jnp.bfloat16))
        row, col = iotas(EXPERTS * MAIN, rows)
        pick_m[...] = one_hot(widened == (row & 15).astype(jnp.float32))
        pick_o[...] = one_hot(ranks == float(MAIN))

    attention_phase(
        q_ref, k_ref, v_ref, attended, qs, ks, vs, ob, attn_recv, attn_send, out_send, out_recv, pump_at, prepare
    )
    load_residual.wait()

    def upright(line):
        return jnp.broadcast_to(line, (rows, rows)).T[:, 0:1]

    state = residual[...].astype(jnp.float32) + attended[...].astype(jnp.float32)
    hidden[...] = state
    own_squares = jnp.sum(state * state, axis=1, keepdims=True)
    squares[tensor] = jnp.broadcast_to(own_squares, (rows, rows)).T[0:8, :]

    def tell(step):
        peer = lax.rem(tensor + step, 4)
        return pltpu.make_async_remote_copy(
            src_ref=squares.at[tensor],
            dst_ref=squares.at[tensor],
            send_sem=sq_send.at[peer],
            recv_sem=sq_recv.at[tensor],
            device_id={"tensor": peer},
            device_id_type=MESH,
        )

    for step in (1, 2, 3):
        tell(step).start()

    pump(1)
    for step in (1, 2, 3):
        peer = lax.rem(tensor + step, 4)
        arrived(squares.at[peer], sq_recv.at[peer])
    total = squares[0] + squares[1] + squares[2] + squares[3]
    inverse = lax.rsqrt(total / D + EPS)
    normed = (hidden[...] * upright(inverse[0:1, :]) * gain_ref[...]).astype(jnp.bfloat16)
    disp_m[...] = exact_dot(pick_m[...], normed).astype(jnp.bfloat16)
    overflow = exact_dot(pick_o[...], normed).astype(jnp.bfloat16)
    pieces = quarter // HD
    stacked = jnp.concatenate(
        [overflow[:, n * HD : (n + 1) * HD] for n in range(pieces)], axis=0
    )
    row, col = iotas(EXPERTS * TILE_ROWS, EXPERTS * pieces)
    shuffle = one_hot((((col & 15) << 4) | (col >> 4)) == row)
    disp_o[...] = exact_dot(shuffle, stacked).astype(jnp.bfloat16)

    def rows_of(number):
        return pl.ds(pl.multiple_of(number * TILE_ROWS, TILE_ROWS), TILE_ROWS)

    def columns_of(number):
        return pl.ds(pl.multiple_of(number * quarter, quarter), quarter)

    def dispatch(step):
        other = lax.rem(rank + step, GROUP)
        pairs = (
            (disp_m.at[rows_of(other), :], xm.at[rows_of(place), columns_of(tensor)]),
            (disp_o.at[rows_of(other), :], xo.at[rows_of(rank), :]),
        )
        return [
            pltpu.make_async_remote_copy(
                src_ref=src,
                dst_ref=dst,
                send_sem=disp_send.at[step, index],
                recv_sem=disp_recv.at[index],
                device_id=member(other),
                device_id_type=MESH,
            )
            for index, (src, dst) in enumerate(pairs)
        ]

    pltpu.make_async_copy(
        disp_m.at[rows_of(rank), :], xm.at[rows_of(place), columns_of(tensor)], disp_recv.at[0]
    ).start()
    pltpu.make_async_copy(
        disp_o.at[rows_of(rank), :], xo.at[rows_of(rank), :], disp_recv.at[1]
    ).start()

    @pl.loop(1, GROUP)
    def _(step):
        for copy in dispatch(step):
            copy.start()

    row, col = iotas(36 * 16, 4 * OVER)
    chunk, inside = col >> 8, col & 255
    source, part, piece = inside >> 6, (inside >> 4) & 3, inside & 15
    goal = (part * pieces + piece) * 16 + chunk * 4 + source
    spread[...] = one_hot(jnp.logical_and(piece < pieces, goal == row))
    row, col = iotas(4 * OVER, 36 * 16)
    chunk, inside = row >> 8, row & 255
    source, part, piece = inside >> 6, (inside >> 4) & 3, inside & 15
    goal = (part * pieces + piece) * 16 + chunk * 4 + source
    gather[...] = one_hot(jnp.logical_and(piece < pieces, goal == col))

    def main(slot):
        return pl.ds(slot * SLOT, SLOT)

    def over(slot):
        return pl.ds(slot * OVER, OVER)

    def pass_on(slot, goal, send_sem, recv_sem, number, device):
        send(xm.at[main(slot), :], xm.at[main(goal), :], send_sem.at[number, 0], recv_sem.at[number, 0], device)
        send(xo.at[over(slot), :], xo.at[over(goal), :], send_sem.at[number, 1], recv_sem.at[number, 1], device)

    def landed(slot, recv_sem, number):
        arrived(xm.at[main(slot), :], recv_sem.at[number, 0])
        arrived(xo.at[over(slot), :], recv_sem.at[number, 1])

    def share(slot):
        pass_on(slot, twin(slot), sibx_send, sibx_recv, CARRIED.index(slot), sibling)

    pump(3)
    arrived(xm.at[main(OWN), :], disp_recv.at[0])
    arrived(xo.at[over(OWN), :], disp_recv.at[1])
    pass_on(OWN, major(1), aga_send, aga_recv, 0, ahead)
    pass_on(OWN, minor(1), agb_send, agb_recv, 0, behind)
    share(OWN)
    def fetch_shared(step):
        low, count = STEPS[step]
        for slot in CARRIED:
            if low <= slot < low + count:
                landed(twin(slot), sibx_recv, CARRIED.index(slot))

    def step_rows(step):
        return STEPS[step][1] * SLOT

    def rows_in(step):
        low = STEPS[step][0] * SLOT
        return jnp.concatenate(
            [xm[low : low + step_rows(step), :], over_x[step * 16 : step * 16 + 16, :]], axis=0
        )

    def gate_products(step):
        low, count = STEPS[step]
        size = step_rows(step) + 16
        tiles = xo[low * OVER : (low + count) * OVER, :]
        stack = exact_dot(spread[:, 0 : count * OVER], tiles).astype(jnp.bfloat16)
        for n in range(36):
            over_x[step * 16 : step * 16 + 16, n * HD : (n + 1) * HD] = stack[n * 16 : (n + 1) * 16, :]
        gates[step * 272 : step * 272 + size, :] = exact_dot(rows_in(step), w1[:, 0:hid_dev])

    def up_products(step):
        size = step_rows(step) + 16
        up = exact_dot(rows_in(step), w1[:, hid_dev : 2 * hid_dev]) * inner[1:2, :]
        gate = gates[step * 272 : step * 272 + size, :] * inner[0:1, :]
        act[step * 272 : step * 272 + size, :] = (gate / (1.0 + jnp.exp(-gate)) * up).astype(
            jnp.bfloat16
        )

    def lanes_of(half, n):
        start = half * half_width + n * 768
        return pl.ds(start if isinstance(n, int) else pl.multiple_of(start, 256), 768)

    def down_part(step, half):
        low, count = STEPS[step]
        size = step_rows(step)

        @pl.loop(0, half_width // 768)
        def _(n):
            lanes = lanes_of(half, n)
            result = exact_dot(act[step * 272 : step * 272 + size + 16, :], wd[:, lanes])
            result = result.astype(jnp.bfloat16)
            ym[low * SLOT : low * SLOT + size, lanes] = result[0:size, :]
            over_y[step * 16 : step * 16 + 16, lanes] = result[size:, :]

        if half:
            stack = jnp.concatenate(
                [over_y[step * 16 : step * 16 + 16, n * HD : (n + 1) * HD] for n in range(36)], axis=0
            )
            yo[low * OVER : (low + count) * OVER, :] = exact_dot(
                gather[0 : count * OVER, :], stack
            ).astype(jnp.bfloat16)
        part = pl.ds(half * half_width, half_width)
        for slot in CARRIED:
            if low <= slot < low + count:
                number = CARRIED.index(slot)
                other = twin(slot)
                send(
                    ym.at[main(other), part],
                    sib_m.at[number, :, part],
                    siby_send.at[number, half],
                    siby_recv.at[number, half],
                    sibling,
                )
                if half:
                    send(
                        yo.at[over(other), :],
                        sib_o.at[number],
                        siby_send.at[number, 2],
                        siby_recv.at[number, 2],
                        sibling,
                    )

    for k in (1, 2, 3):
        pump(6)
        landed(major(k), aga_recv, k - 1)
        pass_on(major(k), major(k + 1), aga_send, aga_recv, k, ahead)
        share(major(k))
        landed(minor(k), agb_recv, k - 1)
        if k < 3:
            pass_on(minor(k), minor(k + 1), agb_send, agb_recv, k, behind)
        share(minor(k))
        if k == 1:
            arrived(gate_part, w_recv.at[0])
        fetch_shared(k - 1)
        gate_products(k - 1)
    fetch_shared(3)
    gate_products(3)
    pump(2 * PIECES - progress[0])
    for index in (1, 4, 5):
        arrived(moved[index][1], w_recv.at[index])
    for line in range(4):
        for n in range(pieces):
            chunk = line * pieces + n
            tall[line * 16 + n : line * 16 + n + 1, :] = wide[0:1, chunk * HD : (chunk + 1) * HD]
        tall[line * 16 + pieces : (line + 1) * 16, :] = jnp.zeros((16 - pieces, HD), jnp.float32)
    for step in (0, 1, 2):
        up_products(step)
        pump(1)
    landed(major(4), aga_recv, 3)
    share(major(4))
    up_products(3)
    pump(1)
    fetch_shared(4)
    gate_products(4)
    up_products(4)
    pump(2 * PIECES + PIECES // 2 - progress[0])
    arrived(down_half[0], w_recv.at[2])

    def summed(own, others):
        value = own.astype(jnp.float32)
        for other in others:
            value = value + other.astype(jnp.float32)
        return value

    def await_parts(slot, extras, half):
        number = CARRIED.index(slot)
        part = pl.ds(half * half_width, half_width)
        arrived(sib_m.at[number, :, part], siby_recv.at[number, half])
        for ref_m, ref_o, spot, sems in extras:
            arrived(ref_m.at[spot, :, part], sems.at[spot, half])
        if half:
            arrived(sib_o.at[number], siby_recv.at[number, 2])
            for ref_m, ref_o, spot, sems in extras:
                arrived(ref_o.at[spot], sems.at[spot, 2])

    def block(slot, extras, lanes):
        number = CARRIED.index(slot)
        return summed(
            ym[main(slot), lanes],
            [sib_m[number, :, lanes]] + [extra[0][extra[2], :, lanes] for extra in extras],
        )

    def tiles(slot, extras):
        number = CARRIED.index(slot)
        return summed(yo[over(slot), :], [sib_o[number]] + [extra[1][extra[2]] for extra in extras])

    def hop(slot, extras, half, goal_m, goal_o, send_sem, recv_sem, number, device):
        await_parts(slot, extras, half)

        @pl.loop(0, half_width // 768)
        def _(n):
            lanes = lanes_of(half, n)
            ym[main(slot), lanes] = block(slot, extras, lanes).astype(jnp.bfloat16)

        part = pl.ds(half * half_width, half_width)
        send(
            ym.at[main(slot), part],
            goal_m.at[number, :, part],
            send_sem.at[number, half],
            recv_sem.at[number, half],
            device,
        )
        if half:
            yo[over(slot), :] = tiles(slot, extras).astype(jnp.bfloat16)
            send(
                yo.at[over(slot), :],
                goal_o.at[number],
                send_sem.at[number, 2],
                recv_sem.at[number, 2],
                device,
            )

    def hop_a(k, half):
        extras = [(rxa_m, rxa_o, k, rsa_recv)] if k < 4 else []
        hop(major(k), extras, half, rxa_m, rxa_o, rsa_send, rsa_recv, k - 1, behind)

    def hop_b(k, half):
        extras = [(rxb_m, rxb_o, k, rsb_recv)] if k < 3 else []
        hop(minor(k), extras, half, rxb_m, rxb_o, rsb_send, rsb_recv, k - 1, ahead)

    def give_back(step, half):
        spot = lax.rem(place + lax.div(step, 2), 4)
        part = 2 * half + lax.rem(tensor + step, 2)
        other = spot * 4 + part
        return other, eo_m.at[rows_of(spot), columns_of(part)], ret_m.at[rows_of(rank), :]

    def give_all(half, start):
        @pl.loop(0, 8)
        def _(step):
            other, src, dst = give_back(step, half)

            @pl.when(other != rank)
            def _():
                copy = pltpu.make_async_remote_copy(
                    src_ref=src,
                    dst_ref=dst,
                    send_sem=ret_send.at[half * 8 + step, 0],
                    recv_sem=ret_recv.at[0],
                    device_id=member(other),
                    device_id_type=MESH,
                )
                if start:
                    copy.start()
                else:
                    copy.wait_send()

            if start:

                @pl.when(other == rank)
                def _():
                    pltpu.make_async_copy(src, dst, ret_recv.at[0]).start()

    def give_over(step):
        other = lax.rem(rank + step, GROUP)
        return pltpu.make_async_remote_copy(
            src_ref=eo_o.at[rows_of(other), :],
            dst_ref=ret_o.at[rows_of(rank), :],
            send_sem=ret_send.at[step, 1],
            recv_sem=ret_recv.at[1],
            device_id=member(other),
            device_id_type=MESH,
        )

    def finish(half):
        last = [(rxb_m, rxb_o, 0, rsb_recv), (rxa_m, rxa_o, 0, rsa_recv)]
        await_parts(OWN, last, half)

        @pl.loop(0, half_width // 768)
        def _(n):
            lanes = lanes_of(half, n)
            eo_m[:, lanes] = (block(OWN, last, lanes) * wide[0:1, lanes]).astype(jnp.bfloat16)

        if half:
            value = tiles(OWN, last)
            for n in range(4):
                eo_o[n * 64 : (n + 1) * 64, :] = (
                    value[n * 64 : (n + 1) * 64, :] * tall[...]
                ).astype(jnp.bfloat16)
        give_all(half, True)
        if half:
            pltpu.make_async_copy(
                eo_o.at[rows_of(rank), :], ret_o.at[rows_of(rank), :], ret_recv.at[1]
            ).start()

            @pl.loop(1, GROUP)
            def _(step):
                give_over(step).start()

    down_part(4, 0)
    hop_a(4, 0)
    down_part(3, 0)
    hop_b(3, 0)
    for step in (2, 1, 0):
        pump(1)
        down_part(step, 0)
    hop_a(3, 0)
    hop_b(2, 0)
    pump(1)
    hop_a(2, 0)
    hop_b(1, 0)
    pump(n_pieces)
    arrived(down_half[1], w_recv.at[3])
    down_part(4, 1)
    hop_a(4, 1)
    down_part(3, 1)
    hop_b(3, 1)
    hop_a(1, 0)
    down_part(2, 1)
    hop_a(3, 1)
    hop_b(2, 1)
    down_part(1, 1)
    hop_a(2, 1)
    hop_b(1, 1)
    down_part(0, 1)
    finish(0)
    hop_a(1, 1)
    finish(1)

    expert_id = iotas(rows, EXPERTS)[1]
    hits = [expert_id == upright(routes_ref[k : k + 1, :]) for k in range(2)]
    first, second = iotas(rows, rows)
    both = one_hot(jnp.logical_or(hits[0], hits[1]))
    token_ranks = exact_dot(one_hot(second < first), both)
    row, col = iotas(EXPERTS, EXPERTS * MAIN)
    expand = one_hot((col >> 4) == row)
    slot_rank = (iotas(rows, EXPERTS * MAIN)[1] & 15).astype(jnp.float32)
    selects = []
    for k in range(2):
        own_ranks = jnp.where(hits[k], token_ranks, -1.0)
        wide_ranks = exact_dot(own_ranks.astype(jnp.bfloat16), expand)
        selects.append((one_hot(wide_ranks == slot_rank), one_hot(own_ranks == float(MAIN))))
    row, col = iotas(EXPERTS * pieces, EXPERTS * TILE_ROWS)
    unshuffle = one_hot((((row & 15) << 4) | (row >> 4)) == col)

    for copy in pending:
        copy.wait_send()
    for step in (1, 2, 3):
        tell(step).wait_send()

    @pl.loop(1, GROUP)
    def _(step):
        for copy in dispatch(step):
            copy.wait_send()

    @pl.when(swapping)
    def _():
        for index in (4, 5):
            swap(index).wait_send()
        for number in range(n_pieces - IN_FLIGHT, n_pieces):
            load(number).wait_send()

    arrived(ret_m, ret_recv.at[0])
    arrived(ret_o, ret_recv.at[1])
    back = exact_dot(unshuffle, ret_o[...]).astype(jnp.bfloat16)
    back = jnp.concatenate(
        [back[n * EXPERTS : (n + 1) * EXPERTS, :] for n in range(pieces)], axis=1
    )
    routed = jnp.zeros((rows, quarter), jnp.float32)
    for k in range(2):
        picked = exact_dot(selects[k][0], ret_m[...]) + exact_dot(selects[k][1], back)
        routed = routed + picked * upright(weight_ref[k : k + 1, :])
    out_ref[...] = (hidden[...] + routed).astype(jnp.bfloat16)

    for half in range(2):
        give_all(half, False)

    @pl.loop(1, GROUP)
    def _(step):
        give_over(step).wait_send()


def layer(
    queries, keys, values, residual, norm_gain, routes, route_weight, w_gate, w_up, w_down, scale_hidden, scale_out
):
    rows, quarter = residual.shape
    _, width, hid_dev = w_gate.shape
    length = rows * N_CTX
    vmem = pl.BlockSpec(memory_space=pltpu.VMEM)
    hbm = pl.BlockSpec(memory_space=pl.ANY)
    half = jnp.bfloat16
    dma = pltpu.SemaphoreType.DMA
    return pl.pallas_call(
        layer_kernel,
        out_shape=jax.ShapeDtypeStruct((rows, quarter), half),
        in_specs=[vmem] * 3 + [hbm] * 9,
        out_specs=vmem,
        scratch_shapes=[
            pltpu.VMEM((rows, quarter), half),
            pltpu.VMEM((rows, quarter), half),
            pltpu.VMEM((length, HD), half),
            pltpu.VMEM((length, HD), half),
            pltpu.VMEM((length, HD), half),
            pltpu.VMEM((length, HD), half),
            pltpu.VMEM((16 * SLOT, width), half),
            pltpu.VMEM((16 * OVER, HD), half),
            pltpu.VMEM((16 * SLOT, width), half),
            pltpu.VMEM((16 * OVER, HD), half),
            pltpu.VMEM((8, SLOT, width), half),
            pltpu.VMEM((8, OVER, HD), half),
            pltpu.VMEM((4, SLOT, width), half),
            pltpu.VMEM((4, OVER, HD), half),
            pltpu.VMEM((3, SLOT, width), half),
            pltpu.VMEM((3, OVER, HD), half),
            pltpu.VMEM((width, 2 * hid_dev), half),
            pltpu.VMEM((hid_dev, width), half),
            pltpu.VMEM((1, width), jnp.float32),
            pltpu.VMEM((2, hid_dev), jnp.float32),
            pltpu.VMEM((64, HD), jnp.float32),
            pltpu.VMEM((5 * 272, hid_dev), half),
            pltpu.VMEM((5 * 272, hid_dev), jnp.float32),
            pltpu.VMEM((rows, quarter), jnp.float32),
            pltpu.VMEM((EXPERTS * MAIN, quarter), half),
            pltpu.VMEM((EXPERTS * TILE_ROWS, HD), half),
            pltpu.VMEM((SLOT, width), half),
            pltpu.VMEM((OVER, HD), half),
            pltpu.VMEM((EXPERTS * MAIN, quarter), half),
            pltpu.VMEM((EXPERTS * TILE_ROWS, HD), half),
            pltpu.VMEM((80, width), half),
            pltpu.VMEM((80, width), half),
            pltpu.VMEM((EXPERTS * MAIN, rows), half),
            pltpu.VMEM((EXPERTS, rows), half),
            pltpu.VMEM((36 * 16, 4 * OVER), half),
            pltpu.VMEM((4 * OVER, 36 * 16), half),
            pltpu.VMEM((4, 8, rows), jnp.float32),
            dma((6,)),
            dma((6,)),
            dma((4,)),
            dma((4,)),
            dma((2,)),
            dma((GROUP, 2)),
            dma((4, 2)),
            dma((4, 2)),
            dma((3, 2)),
            dma((3, 2)),
            dma((8, 2)),
            dma((8, 2)),
            dma((8, 3)),
            dma((8, 3)),
            dma((4, 3)),
            dma((4, 3)),
            dma((3, 3)),
            dma((3, 3)),
            dma((2,)),
            dma((GROUP, 2)),
            dma((3 * PIECES,)),
            dma((3,)),
            dma((HEADS_HERE, 3)),
            dma((N_CTX,)),
            dma,
            dma,
        ],
        compiler_params=pltpu.CompilerParams(
            collective_id=0, has_side_effects=True, vmem_limit_bytes=60 * 1024 * 1024
        ),
        cost_estimate=pl.CostEstimate(
            flops=6 * 1088 * width * hid_dev + 2 * length * length * HD, bytes_accessed=12 * 10**6, transcendentals=10**6
        ),
    )(
        norm_gain.reshape(1, quarter),
        routes.T,
        route_weight.T,
        residual,
        queries,
        keys,
        values,
        w_gate,
        w_up,
        w_down,
        scale_hidden,
        scale_out,
    )


def solution(mesh):
    in_specs = (
        P(("dp", "context"), "tensor"),
        P(("dp", "context"), "tensor"),
        P(("dp", "context"), "tensor"),
        P(("dp", "context"), "tensor"),
        P("tensor"),
        P(("dp", "context"), None),
        P(("dp", "context"), None),
        P(("dp", "tensor"), None, "context"),
        P(("dp", "tensor"), None, "context"),
        P(("dp", "tensor"), "context", None),
        P(("dp", "tensor"), None, "context"),
        P(("dp", "tensor"), None),
    )
    out_specs = P(("dp", "context"), "tensor")
    return jax.shard_map(layer, mesh=mesh, in_specs=in_specs, out_specs=out_specs, check_vma=False)
```
